512 devices in a mesh: req: 32 (over x, y), sp: 16 (over z, core).
Axes of the slice: x: 4, y: 8, z: 8, core: 2. Of those that a mesh axis runs over, the one named last changes fastest.
Arguments:
- tokens: bfloat16 [23040, 64], P(('req', 'sp')), parts along dimension 0, may hold values from -6 to 6
- strip_rows: int32 [16], replicated, may hold values from 1 to 9, 90 in all
- first_filter: bfloat16 [3, 3, 3, 16, 384], replicated, may hold values from -0.3125 to 0.3125
- first_bias: float32 [384], replicated, may hold values from -3 to 3
- norm_gain: float32 [384], replicated, may hold values from 0.25 to 1.75
- second_filter: bfloat16 [3, 3, 3, 384, 384], P(None, None, None, None, 'sp'), may hold values from -0.0625 to 0.0625
- second_bias: float32 [384], replicated, may hold values from -3 to 3
Outputs:
- strips: bfloat16 [512, 2, 9, 16, 384], P(('req', 'sp')), parts along dimension 0
The draws below stay inside these ranges and needn't reach their ends.
There are 32 independent parts, one for each index of `req`. The reference program is written for one: setup_inputs(seed, part) draws one part's arguments, and reference() takes and returns one part's arrays. A program takes and returns all parts, laid end to end along the dimension named above; an argument that names none is the same for every part. Nothing has to cross between parts.
Inputs may be any that keep to these rules, and one draw needn't show every extreme that they name: `strip_rows`: the lengths sum to 90; the largest is exactly 9 in every draw.
All inputs are finite; a program needn't handle non-finite values.
Results may differ from the reference program's by a relative error of at most 0.0037.
Values may be sent and summed in bfloat16 or wider, within the bound.
A program may use at most 64 MiB of HBM per device.

```python
import math
import jax
import jax.numpy as jnp
import numpy as np
from jax import lax

C = 16
C2 = 384
FR = 2
PH = 45
PW = 8
FEAT = 64
S = 720
MOST = 9
N_SP = 16


def block_scale(key, dims, cuts, least, high):
    factor_of = 1.0
    for dim, shards_of in cuts:
        draws = jax.random.uniform(jax.random.fold_in(jax.random.fold_in(key, 6), dim), (shards_of,), jnp.float32, least / len(cuts), high / len(cuts))
        factor_of = factor_of * jnp.repeat(jnp.exp(draws), dims[dim] // shards_of).reshape((-1,) + (1,) * (len(dims) - 1 - dim))
    return factor_of


def profile(number_of, total, reach, slope):
    loads = [(1 << 20) // math.isqrt(standing ** slope) + 1 for standing in range(2, number_of + 1)]
    surplus, given = total - reach - (number_of - 1), [1] * (number_of - 1)
    while surplus > 0:
        movable = [i for i in range(number_of - 1) if given[i] < reach]
        whole, left = sum([loads[i] for i in movable]), surplus
        for i in movable:
            more = min(reach - given[i], max(1, left * loads[i] // whole), surplus)
            given[i] = given[i] + more
            surplus = surplus - more
    return np.array([reach] + given)


def uneven_parts(own_key, amount, total, reach, skew):
    if amount == 2:
        one = jax.random.randint(own_key, (), max(1, total - reach), min(reach, total - 1) + 1)
        return jnp.stack([one, total - one])
    tallies = jnp.asarray(profile(amount, total, reach, skew), jnp.int32)
    pairs = (amount - 1) // 2
    source_of, taker = tallies[1:1 + 2 * pairs:2], tallies[2:2 + 2 * pairs:2]
    room = jnp.minimum(source_of - 1, reach - taker)
    passed = jax.random.randint(jax.random.fold_in(own_key, 1), (pairs,), 0, 1 << 20) % (room + 1)
    tallies = tallies.at[1:1 + 2 * pairs:2].set(source_of - passed).at[2:2 + 2 * pairs:2].set(taker + passed)
    return tallies[jax.random.permutation(jax.random.fold_in(own_key, 2), amount)]


def scatter_about(own_key, dims, spread, limit, cuts=(), held_as=jnp.bfloat16):
    drawn = spread * jax.random.normal(own_key, dims, jnp.float32)
    if cuts:
        drawn = drawn * block_scale(own_key, dims, cuts, -0.22, 0.18)
    return jnp.clip(drawn, -limit, limit).astype(held_as)


def setup_inputs(seed: int = 0, part: int = 0) -> dict:
    arg_keys = jax.random.split(jax.random.key(seed), 8)
    own_keys = jax.random.split(jax.random.fold_in(arg_keys[7], part), 8)
    tokens = scatter_about(own_keys[0], (S, FEAT), 1.0, 6.0, ((0, 16),))
    strip_rows = uneven_parts(arg_keys[1], N_SP, 2 * PH, MOST, 2).astype(jnp.int32)
    first_filter = scatter_about(arg_keys[2], (3, 3, 3, C, C2), (27 * C) ** -0.5, 0.3125)
    first_bias = scatter_about(arg_keys[3], (C2,), 0.5, 3.0, (), jnp.float32)
    norm_gain = jnp.clip(1.0 + 0.15 * jax.random.normal(arg_keys[4], (C2,), jnp.float32), 0.25, 1.75)
    second_filter = scatter_about(arg_keys[5], (3, 3, 3, C2, C2), (27 * C2) ** -0.5, 0.0625, ((4, 16),))
    second_bias = scatter_about(arg_keys[6], (C2,), 0.5, 3.0, (), jnp.float32)
    return dict(tokens=tokens, strip_rows=strip_rows, first_filter=first_filter, first_bias=first_bias, norm_gain=norm_gain, second_filter=second_filter, second_bias=second_bias)


def arrange(flat):
    grid = flat.reshape(FR, PH, PW, 2, 2, C)
    grid = jnp.transpose(grid, (0, 1, 3, 2, 4, 5))
    return grid.reshape(FR, 2 * PH, 2 * PW, C)

def causal_conv(field, filters, row_pad):
    return lax.conv_general_dilated(field[None], filters, (1, 1, 1), [(2, 0), row_pad, (1, 1)], dimension_numbers=('NDHWC', 'DHWIO', 'NDHWC'), preferred_element_type=jnp.float32)[0]

def activate(first, norm_gain):
    scale = lax.rsqrt(lax.optimization_barrier(jnp.mean(first * first, axis=-1, keepdims=True)) + 1e-06)
    return jax.nn.silu(first * scale * norm_gain).astype(jnp.bfloat16)

def reference(tokens, strip_rows, first_filter, first_bias, norm_gain, second_filter, second_bias):
    latent = arrange(tokens)
    first = causal_conv(latent, first_filter, (1, 1)) + first_bias
    hidden = activate(first, norm_gain)
    final = (causal_conv(hidden, second_filter, (1, 1)) + second_bias).astype(jnp.bfloat16)
    padded = jnp.pad(final, ((0, 0), (0, MOST), (0, 0), (0, 0)))
    starts = (jnp.cumsum(strip_rows) - strip_rows).astype(jnp.int32)

    def place(start, count):
        piece = lax.dynamic_slice_in_dim(padded, start, MOST, 1)
        keep = jnp.arange(MOST, dtype=jnp.int32) < count
        return jnp.where(keep[None, :, None, None], piece, jnp.zeros_like(piece))
    return jax.vmap(place)(starts, strip_rows)
```

```python
import jax
import jax.numpy as jnp
from jax import lax
from jax.experimental import pallas as pl
from jax.experimental.pallas import tpu as pltpu
from jax.sharding import PartitionSpec as P

C = 16
FR = 2
PH = 45
PW = 8
N = 16
TOK = FR * PH * PW // N
HALF = 32
FL = 384
LIVE = PH * PW
C2 = 384
CO = 24
TILES = 13
BLK = 32
CHUNK = 256
MESH = pl.DeviceIdType.MESH
F32, BF16 = jnp.float32, jnp.bfloat16


def peer(i):
    return {"sp": i}


def step_of(t):
    up = (t + 1) // 2
    return 8 + up * (1 - 2 * ((t + 1) % 2))


def col_iota(shape):
    return lax.broadcasted_iota(jnp.int32, shape, len(shape) - 1)


def row_iota(shape):
    return lax.broadcasted_iota(jnp.int32, shape, len(shape) - 2)


def shift_of(phase, d):
    moved = phase + d
    return moved % 2, moved // 2


def prepare(f_ref, b1_ref, gain_ref, b2_ref, me, ft, ft0, ghalf, b2col, place, xp):
    tap1, tap2 = f_ref[0].astype(F32), f_ref[1].astype(F32)
    bias = b1_ref[...]
    hi = bias.astype(BF16).astype(F32)
    mid = (bias - hi).astype(BF16).astype(F32)
    low = bias - hi - mid
    rows = row_iota((16, C2))
    bias_rows = jnp.where(rows == 0, hi, jnp.where(rows == 1, mid, jnp.where(rows == 2, low, 0.0)))
    ft[...] = jnp.concatenate([tap2, bias_rows, tap1, jnp.zeros((80, C2), F32)], 0).T[:, :304].astype(BF16)
    ft0[...] = jnp.concatenate([bias_rows, tap2, jnp.zeros((96, C2), F32)], 0).T[:, :160].astype(BF16)
    ghalf[...] = jnp.broadcast_to(gain_ref[...] * 0.5, (128, C2)).T
    b2col[...] = jnp.broadcast_to(b2_ref[...], (128, C2)).T
    shape = (256, FL)
    token = row_iota(shape)
    src, i = token // HALF, token % HALF
    lane = col_iota(shape)
    one, zero = jnp.ones(shape, F32), jnp.zeros(shape, F32)
    place[0] = jnp.where(lane == src * TOK + i, one, zero).astype(BF16)
    place[1] = jnp.where((lane == src * TOK + HALF + i) & (i < TOK - HALF), one, zero).astype(BF16)
    xp[144:160, :] = jnp.ones((16, 4 * FL), BF16)


def patches(tok_all, place, xp):
    halves = [tok_all[8 * f:8 * f + 8].reshape(256, 128).astype(F32).T.astype(BF16) for f in range(FR)]
    left = jnp.concatenate([h[:64] for h in halves], 0)
    right = jnp.concatenate([h[64:] for h in halves], 0)
    grid = jnp.dot(left, place[0], preferred_element_type=F32) + jnp.dot(right, place[1], preferred_element_type=F32)
    q = col_iota((1, FL)) % PW
    for f in range(FR):
        for a2 in range(2):
            for b2 in range(2):
                at = f * 64 + (a2 * 2 + b2) * C
                field = grid[at:at + C]
                moved = {}
                for sr in ((0, -1) if a2 == 1 else (0, 1)):
                    for sq in ((0, -1) if b2 == 1 else (0, 1)):
                        piece = field
                        if sr or sq:
                            piece = pltpu.roll(piece, (-(PW * sr + sq)) % FL, 1)
                        if sq:
                            piece = jnp.where(q == (0 if sq < 0 else PW - 1), 0.0, piece)
                        moved[sr, sq] = piece.astype(BF16)
                for a in range(2):
                    for b in range(2):
                        for dy in range(3):
                            for dx in range(3):
                                sa, sr = shift_of(a, dy - 1)
                                sb, sq = shift_of(b, dx - 1)
                                if (sa, sb) == (a2, b2):
                                    row = (160 if f == 0 else 0) + (dy * 3 + dx) * C
                                    ph = a * 2 + b
                                    xp[row:row + C, ph * FL:(ph + 1) * FL] = moved[sr, sq]


def convolve(f, xp, ft, ft0, ghalf, wcat, hid, prod):
    for at in range(0, 4 * FL, CHUNK):
        lanes = slice(at, at + CHUNK)
        if f == 0:
            first = jnp.dot(ft0[...], xp[144:304, lanes], preferred_element_type=F32)
        else:
            first = jnp.dot(ft[...], xp[:, lanes], preferred_element_type=F32)
        mean = jnp.sum(first * first, axis=0, keepdims=True) * (1.0 / C2)
        live = (col_iota((1, CHUNK)) + at) % FL < LIVE
        scale = jnp.where(live, lax.rsqrt(mean + 1e-6), 0.0)
        gain = jnp.concatenate([ghalf[...]] * (CHUNK // 128), 1)
        u = first * scale * gain
        h = (u + u * jnp.tanh(u)).astype(BF16)
        hid[f * C2:(f + 1) * C2, lanes] = h
        if f == 0:
            prod[:, lanes] = jnp.dot(wcat[:, C2:], h, preferred_element_type=F32)
        else:
            prod[:, lanes] = jnp.dot(wcat[...], hid[:, lanes], preferred_element_type=F32)


def gather_taps(f, me, prod, b2col, fin):
    q = col_iota((1, FL)) % PW
    bias = b2col[pl.ds(pl.multiple_of(me * CO, 8), CO), :]
    bias = jnp.concatenate([bias] * (FL // 128), 1)
    outs = []
    for a in range(2):
        for b in range(2):
            sums = {}
            for dy in range(3):
                for dx in range(3):
                    sa, sr = shift_of(a, dy - 1)
                    sb, sq = shift_of(b, dx - 1)
                    tap, ph = dy * 3 + dx, sa * 2 + sb
                    term = prod[tap * CO:(tap + 1) * CO, ph * FL:(ph + 1) * FL]
                    sums[sr, sq] = sums[sr, sq] + term if (sr, sq) in sums else term
            sr, sq = (-1, 1)[a], (-1, 1)[b]
            side = sums[0, sq] + pltpu.roll(sums[sr, sq], (-PW * sr) % FL, 1)
            side = pltpu.roll(side, (-sq) % FL, 1)
            side = jnp.where(q == (0 if sq < 0 else PW - 1), 0.0, side)
            outs.append(sums[0, 0] + pltpu.roll(sums[sr, 0], (-PW * sr) % FL, 1) + side + bias)
    block = col_iota((1, 128)) // 32
    for t in range(FL // 128):
        for j in range(4):
            tile = None
            for ph in range(4):
                piece = outs[ph][:, 128 * t:128 * t + 128]
                if ph != j:
                    piece = pltpu.roll(piece, (32 * (ph - j)) % 128, 1)
                tile = piece if tile is None else jnp.where(block == ph, piece, tile)
            fin[f, 4 * t + j] = tile
    fin[f, TILES - 1] = jnp.zeros((CO, 128), F32)


def strip_block(f, start, fin):
    r0 = start // 2
    tile, off = r0 // 4, r0 % 4
    one, two = fin[f, tile], fin[f, tile + 1]
    row = (col_iota((1, 128)) % 32) // PW
    two = pltpu.roll(two, (32 - PW * off) % 128, 1)
    main = jnp.where(row + off < 4, pltpu.roll(one, (128 - PW * off) % 128, 1), two)
    fifth = pltpu.roll(two, 96, 1)
    packed = jnp.where(row == 0, fifth[:8], jnp.where(row == 1, pltpu.roll(fifth[8:16], PW, 1), pltpu.roll(fifth[16:], 2 * PW, 1)))
    return jnp.concatenate([main, packed], 0).astype(BF16)


def main_kernel(
    rows_ref, tok_ref, f_ref, b1_ref, gain_ref, w_ref, b2_ref, recv,
    tokv, fv, b1v, gainv, b2v, pack, tok_all, ft, ft0, ghalf, b2col, place, wcat, xp, hid, prod, fin, send, starts,
    local_sem, tok_send, tok_recv, out_send, out_recv,
):
    me = lax.axis_index("sp")
    barrier = pltpu.get_barrier_semaphore()

    def greet(i, carry):
        pl.semaphore_signal(barrier, inc=1, device_id=peer(lax.rem(me + i, N)), device_id_type=MESH)
        return carry

    lax.fori_loop(1, N, greet, 0)

    copies = [
        (tok_ref, tokv), (f_ref.at[1], fv.at[0]), (f_ref.at[2], fv.at[1]), (b1_ref, b1v), (gain_ref, gainv), (b2_ref, b2v),
        (w_ref.at[1], wcat.at[:, 0:C2]), (w_ref.at[2], wcat.at[:, C2:2 * C2]),
    ]
    copies = [pltpu.make_async_copy(s, d, local_sem.at[i]) for i, (s, d) in enumerate(copies)]
    for copy in copies:
        copy.start()

    def begin(i, start):
        starts[i] = start
        return start + rows_ref[i]

    lax.fori_loop(0, N, begin, 0)

    copies[0].wait()
    tokens = tokv[...].astype(F32)
    right = jnp.concatenate([tokens[HALF:], jnp.zeros((2 * HALF - TOK, 64), F32)], 0)
    block = jnp.concatenate([tokens[:HALF], right], 1).astype(BF16)
    pack[...] = block
    tok_all[me] = block
    pl.semaphore_wait(barrier, N - 1)

    def tok_copy(to, src):
        return pltpu.make_async_remote_copy(
            src_ref=pack, dst_ref=tok_all.at[src], send_sem=tok_send.at[to], recv_sem=tok_recv.at[src],
            device_id=peer(to), device_id_type=MESH,
        )

    def tok_start(t, carry):
        tok_copy(lax.rem(me + step_of(t), N), me).start()
        return carry

    lax.fori_loop(0, N - 1, tok_start, 0)

    for copy in copies[1:]:
        copy.wait()
    prepare(fv, b1v, gainv, b2v, me, ft, ft0, ghalf, b2col, place, xp)

    def tok_wait(i, carry):
        src = lax.rem(me + i, N)
        tok_copy(src, src).wait_recv()
        return carry

    lax.fori_loop(1, N, tok_wait, 0)
    patches(tok_all, place, xp)

    def out_copy(f, to, src):
        return pltpu.make_async_remote_copy(
            src_ref=send.at[f, to], dst_ref=recv.at[src, f], send_sem=out_send.at[f, to], recv_sem=out_recv.at[f, src],
            device_id=peer(to), device_id_type=MESH,
        )

    for f in range(FR):
        convolve(f, xp, ft, ft0, ghalf, wcat, hid, prod)
        gather_taps(f, me, prod, b2col, fin)

        def out_start(t, carry):
            to = lax.rem(me + step_of(t), N)
            send[f, to] = strip_block(f, starts[to], fin)
            out_copy(f, to, me).start()
            return carry

        lax.fori_loop(0, N - 1, out_start, 0)
        recv[me, f] = strip_block(f, starts[me], fin)

    def out_wait(i, carry):
        other = lax.rem(me + i, N)
        for f in range(FR):
            out_copy(f, other, other).wait()
        tok_copy(other, other).wait_send()
        return carry

    lax.fori_loop(1, N, out_wait, 0)


def exchange(strip_rows, tokens, f, b1, gain, w, b2):
    anywhere = pl.BlockSpec(memory_space=pl.ANY)
    return pl.pallas_call(
        main_kernel,
        out_shape=pltpu.VMEM((N, FR, BLK, 128), BF16),
        in_specs=[pl.BlockSpec(memory_space=pltpu.SMEM)] + [anywhere] * 6,
        out_specs=pl.BlockSpec(memory_space=pltpu.VMEM),
        scratch_shapes=[
            pltpu.VMEM((TOK, 64), BF16),
            pltpu.VMEM((2, 144, C2), BF16),
            pltpu.VMEM((1, C2), F32),
            pltpu.VMEM((1, C2), F32),
            pltpu.VMEM((1, C2), F32),
            pltpu.VMEM((HALF, 128), BF16),
            pltpu.VMEM((N, HALF, 128), BF16),
            pltpu.VMEM((C2, 304), BF16),
            pltpu.VMEM((C2, 160), BF16),
            pltpu.VMEM((C2, 128), F32),
            pltpu.VMEM((C2, 128), F32),
            pltpu.VMEM((2, 256, FL), BF16),
            pltpu.VMEM((9 * CO, 2 * C2), BF16),
            pltpu.VMEM((304, 4 * FL), BF16),
            pltpu.VMEM((2 * C2, 4 * FL), BF16),
            pltpu.VMEM((9 * CO, 4 * FL), F32),
            pltpu.VMEM((FR, TILES, CO, 128), F32),
            pltpu.VMEM((FR, N, BLK, 128), BF16),
            pltpu.SMEM((N,), jnp.int32),
            pltpu.SemaphoreType.DMA((8,)),
            pltpu.SemaphoreType.DMA((N,)),
            pltpu.SemaphoreType.DMA((N,)),
            pltpu.SemaphoreType.DMA((FR, N)),
            pltpu.SemaphoreType.DMA((FR, N)),
        ],
        compiler_params=pltpu.CompilerParams(collective_id=0, has_side_effects=True, vmem_limit_bytes=40 << 20),
    )(strip_rows, tokens, f, b1, gain, w, b2)


def assemble_kernel(rows_ref, recv, out):
    me = lax.axis_index("sp")

    def begin(i, start):
        return start + jnp.where(i < me, rows_ref[i], 0)

    start = lax.fori_loop(0, N, begin, 0)
    count = rows_ref[me]
    shape = (9 * 16, 256)
    p, lane = row_iota(shape), col_iota(shape)
    k, col = p // 16, p % 16
    odd = start % 2
    row = odd + k
    phase = (row % 2) * 2 + col % 2
    patch_row = row // 2
    at = phase * 32 + col // 2 + jnp.where(patch_row < 4, patch_row * PW, 128)
    pick = jnp.where((lane == at) & (k < count), 1.0, 0.0).astype(BF16)
    for f in range(FR):
        block = recv[:, f].astype(F32)
        main = block[:, :CO].reshape(C2, 128)
        tail = block[:, CO:]
        tail = jnp.concatenate([tail, pltpu.roll(tail, 128 - PW, 2), pltpu.roll(tail, 128 - 2 * PW, 2)], 1).reshape(C2, 128)
        both = jnp.concatenate([main, tail], 1).astype(BF16)
        strip = lax.dot_general(pick, both, (((1,), (1,)), ((), ())), preferred_element_type=F32)
        out[0, f] = strip.astype(BF16).reshape(9, 16, C2)


def assemble(strip_rows, recv):
    return pl.pallas_call(
        assemble_kernel,
        out_shape=jax.ShapeDtypeStruct((1, FR, 9, 16, C2), BF16),
        in_specs=[pl.BlockSpec(memory_space=pltpu.SMEM), pl.BlockSpec(memory_space=pltpu.VMEM)],
        out_specs=pl.BlockSpec(memory_space=pltpu.VMEM),
        compiler_params=pltpu.CompilerParams(vmem_limit_bytes=20 << 20),
    )(strip_rows, recv)


def per_device(tokens, strip_rows, first_filter, first_bias, norm_gain, second_filter, second_bias):
    f = first_filter.reshape(3, 9 * C, C2)
    w = jnp.transpose(second_filter, (0, 1, 2, 4, 3)).reshape(3, 9 * CO, C2)
    row = lambda v: v.reshape(1, C2)
    recv = exchange(strip_rows, tokens, f, row(first_bias), row(norm_gain), w, row(second_bias))
    return assemble(strip_rows, recv)


def solution(mesh):
    in_specs = (P(("req", "sp"), None), P(), P(), P(), P(), P(None, None, None, None, "sp"), P())
    out_specs = P(("req", "sp"), None, None, None, None)
    return jax.shard_map(
        per_device, mesh=mesh, in_specs=in_specs, out_specs=out_specs, check_vma=False
    )
```

```python
import jax
import jax.numpy as jnp
from jax import lax
from jax.experimental import pallas as pl
from jax.experimental.pallas import tpu as pltpu
from jax.sharding import PartitionSpec as P

C = 16
FR = 2
PH = 45
PW = 8
N = 16
TOK = FR * PH * PW // N
HALF = 32
FL = 384
LIVE = PH * PW
C2 = 384
CO = 24
TILES = 13
BLK = 32
CHUNK = 256
MESH = pl.DeviceIdType.MESH
F32, BF16 = jnp.float32, jnp.bfloat16


def peer(i):
    return {"sp": i}


def step_of(t):
    up = (t + 1) // 2
    return 8 + up * (1 - 2 * ((t + 1) % 2))


def col_iota(shape):
    return lax.broadcasted_iota(jnp.int32, shape, len(shape) - 1)


def row_iota(shape):
    return lax.broadcasted_iota(jnp.int32, shape, len(shape) - 2)


def shift_of(phase, d):
    moved = phase + d
    return moved % 2, moved // 2


def prepare(f_ref, b1_ref, gain_ref, b2_ref, me, ft, ft0, ghalf, b2col, place, xp):
    tap1, tap2 = f_ref[0].astype(F32), f_ref[1].astype(F32)
    bias = b1_ref[...]
    hi = bias.astype(BF16).astype(F32)
    mid = (bias - hi).astype(BF16).astype(F32)
    low = bias - hi - mid
    rows = row_iota((16, C2))
    bias_rows = jnp.where(rows == 0, hi, jnp.where(rows == 1, mid, jnp.where(rows == 2, low, 0.0)))
    ft[...] = jnp.concatenate([tap2, bias_rows, tap1, jnp.zeros((80, C2), F32)], 0).T[:, :304].astype(BF16)
    ft0[...] = jnp.concatenate([bias_rows, tap2, jnp.zeros((96, C2), F32)], 0).T[:, :160].astype(BF16)
    ghalf[...] = jnp.broadcast_to(gain_ref[...] * 0.5, (128, C2)).T
    b2col[...] = jnp.broadcast_to(b2_ref[...], (128, C2)).T
    shape = (256, FL)
    token = row_iota(shape)
    src, i = token // HALF, token % HALF
    lane = col_iota(shape)
    one, zero = jnp.ones(shape, F32), jnp.zeros(shape, F32)
    place[0] = jnp.where(lane == src * TOK + i, one, zero).astype(BF16)
    place[1] = jnp.where((lane == src * TOK + HALF + i) & (i < TOK - HALF), one, zero).astype(BF16)
    xp[144:160, :] = jnp.ones((16, 4 * FL), BF16)


def patches(tok_all, place, xp):
    halves = [tok_all[8 * f:8 * f + 8].reshape(256, 128).astype(F32).T.astype(BF16) for f in range(FR)]
    left = jnp.concatenate([h[:64] for h in halves], 0)
    right = jnp.concatenate([h[64:] for h in halves], 0)
    grid = jnp.dot(left, place[0], preferred_element_type=F32) + jnp.dot(right, place[1], preferred_element_type=F32)
    q = col_iota((1, FL)) % PW
    for f in range(FR):
        for a2 in range(2):
            for b2 in range(2):
                at = f * 64 + (a2 * 2 + b2) * C
                field = grid[at:at + C]
                moved = {}
                for sr in ((0, -1) if a2 == 1 else (0, 1)):
                    for sq in ((0, -1) if b2 == 1 else (0, 1)):
                        piece = field
                        if sr or sq:
                            piece = pltpu.roll(piece, (-(PW * sr + sq)) % FL, 1)
                        if sq:
                            piece = jnp.where(q == (0 if sq < 0 else PW - 1), 0.0, piece)
                        moved[sr, sq] = piece.astype(BF16)
                for a in range(2):
                    for b in range(2):
                        for dy in range(3):
                            for dx in range(3):
                                sa, sr = shift_of(a, dy - 1)
                                sb, sq = shift_of(b, dx - 1)
                                if (sa, sb) == (a2, b2):
                                    row = (160 if f == 0 else 0) + (dy * 3 + dx) * C
                                    ph = a * 2 + b
                                    xp[row:row + C, ph * FL:(ph + 1) * FL] = moved[sr, sq]


def convolve(f, xp, ft, ft0, ghalf, wcat, hid, prod):
    for at in range(0, 4 * FL, CHUNK):
        lanes = slice(at, at + CHUNK)
        if f == 0:
            first = jnp.dot(ft0[...], xp[144:304, lanes], preferred_element_type=F32)
        else:
            first = jnp.dot(ft[...], xp[:, lanes], preferred_element_type=F32)
        mean = jnp.sum(first * first, axis=0, keepdims=True) * (1.0 / C2)
        live = (col_iota((1, CHUNK)) + at) % FL < LIVE
        scale = jnp.where(live, lax.rsqrt(mean + 1e-6), 0.0)
        gain = jnp.concatenate([ghalf[...]] * (CHUNK // 128), 1)
        u = first * scale * gain
        h = (u + u * jnp.tanh(u)).astype(BF16)
        hid[f * C2:(f + 1) * C2, lanes] = h
        if f == 0:
            prod[:, lanes] = jnp.dot(wcat[:, C2:], h, preferred_element_type=F32)
        else:
            prod[:, lanes] = jnp.dot(wcat[...], hid[:, lanes], preferred_element_type=F32)


def gather_taps(f, me, prod, b2col, fin):
    q = col_iota((1, FL)) % PW
    bias = b2col[pl.ds(pl.multiple_of(me * CO, 8), CO), :]
    bias = jnp.concatenate([bias] * (FL // 128), 1)
    outs = []
    for a in range(2):
        for b in range(2):
            sums = {}
            for dy in range(3):
                for dx in range(3):
                    sa, sr = shift_of(a, dy - 1)
                    sb, sq = shift_of(b, dx - 1)
                    tap, ph = dy * 3 + dx, sa * 2 + sb
                    term = prod[tap * CO:(tap + 1) * CO, ph * FL:(ph + 1) * FL]
                    sums[sr, sq] = sums[sr, sq] + term if (sr, sq) in sums else term
            sr, sq = (-1, 1)[a], (-1, 1)[b]
            side = sums[0, sq] + pltpu.roll(sums[sr, sq], (-PW * sr) % FL, 1)
            side = pltpu.roll(side, (-sq) % FL, 1)
            side = jnp.where(q == (0 if sq < 0 else PW - 1), 0.0, side)
            outs.append(sums[0, 0] + pltpu.roll(sums[sr, 0], (-PW * sr) % FL, 1) + side + bias)
    block = col_iota((1, 128)) // 32
    for t in range(FL // 128):
        for j in range(4):
            tile = None
            for ph in range(4):
                piece = outs[ph][:, 128 * t:128 * t + 128]
                if ph != j:
                    piece = pltpu.roll(piece, (32 * (ph - j)) % 128, 1)
                tile = piece if tile is None else jnp.where(block == ph, piece, tile)
            fin[f, 4 * t + j] = tile
    fin[f, TILES - 1] = jnp.zeros((CO, 128), F32)


def strip_block(f, start, fin):
    r0 = start // 2
    tile, off = r0 // 4, r0 % 4
    one, two = fin[f, tile], fin[f, tile + 1]
    row = (col_iota((1, 128)) % 32) // PW
    two = pltpu.roll(two, (32 - PW * off) % 128, 1)
    main = jnp.where(row + off < 4, pltpu.roll(one, (128 - PW * off) % 128, 1), two)
    fifth = pltpu.roll(two, 96, 1)
    packed = jnp.where(row == 0, fifth[:8], jnp.where(row == 1, pltpu.roll(fifth[8:16], PW, 1), pltpu.roll(fifth[16:], 2 * PW, 1)))
    return jnp.concatenate([main, packed], 0).astype(BF16)


def main_kernel(
    rows_ref, tok_ref, f_ref, b1_ref, gain_ref, w_ref, b2_ref, recv,
    rows, tokv, fv, b1v, gainv, b2v, pack, tok_all, ft, ft0, ghalf, b2col, place, wcat, xp, hid, prod, fin, send, starts,
    local_sem, tok_send, tok_recv, out_send, out_recv,
):
    me = lax.axis_index("sp")
    barrier = pltpu.get_barrier_semaphore()

    def greet(i, carry):
        pl.semaphore_signal(barrier, inc=1, device_id=peer(lax.rem(me + i, N)), device_id_type=MESH)
        return carry

    lax.fori_loop(1, N, greet, 0)

    copies = [
        (tok_ref, tokv), (f_ref.at[1], fv.at[0]), (f_ref.at[2], fv.at[1]), (b1_ref, b1v.at[0]), (gain_ref, gainv.at[0]), (b2_ref, b2v.at[0]),
        (w_ref.at[1], wcat.at[:, 0:C2]), (w_ref.at[2], wcat.at[:, C2:2 * C2]), (rows_ref, rows),
    ]
    copies = [pltpu.make_async_copy(s, d, local_sem.at[i]) for i, (s, d) in enumerate(copies)]
    for copy in copies:
        copy.start()

    copies[0].wait()
    tokens = tokv[...].astype(F32)
    right = jnp.concatenate([tokens[HALF:], jnp.zeros((2 * HALF - TOK, 64), F32)], 0)
    block = jnp.concatenate([tokens[:HALF], right], 1).astype(BF16)
    pack[...] = block
    tok_all[me] = block
    pl.semaphore_wait(barrier, N - 1)

    def tok_copy(to, src):
        return pltpu.make_async_remote_copy(
            src_ref=pack, dst_ref=tok_all.at[src], send_sem=tok_send.at[to], recv_sem=tok_recv.at[src],
            device_id=peer(to), device_id_type=MESH,
        )

    def tok_start(t, carry):
        tok_copy(lax.rem(me + step_of(t), N), me).start()
        return carry

    lax.fori_loop(0, N - 1, tok_start, 0)

    for copy in copies[1:]:
        copy.wait()

    def begin(i, start):
        starts[i] = start
        return start + rows[i]

    lax.fori_loop(0, N, begin, 0)
    prepare(fv, b1v, gainv, b2v, me, ft, ft0, ghalf, b2col, place, xp)

    def tok_wait(i, carry):
        src = lax.rem(me + i, N)
        tok_copy(src, src).wait_recv()
        return carry

    lax.fori_loop(1, N, tok_wait, 0)
    patches(tok_all, place, xp)

    def out_copy(f, to, src):
        return pltpu.make_async_remote_copy(
            src_ref=send.at[f, to], dst_ref=recv.at[src, f], send_sem=out_send.at[f, to], recv_sem=out_recv.at[f, src],
            device_id=peer(to), device_id_type=MESH,
        )

    for f in range(FR):
        convolve(f, xp, ft, ft0, ghalf, wcat, hid, prod)
        gather_taps(f, me, prod, b2col, fin)

        def out_start(t, carry):
            to = lax.rem(me + step_of(t), N)
            send[f, to] = strip_block(f, starts[to], fin)
            out_copy(f, to, me).start()
            return carry

        lax.fori_loop(0, N - 1, out_start, 0)
        recv[me, f] = strip_block(f, starts[me], fin)

    def out_wait(i, carry):
        other = lax.rem(me + i, N)
        for f in range(FR):
            out_copy(f, other, other).wait()
        tok_copy(other, other).wait_send()
        return carry

    lax.fori_loop(1, N, out_wait, 0)


def exchange(strip_rows, tokens, f, b1, gain, w, b2):
    hbm = pl.BlockSpec(memory_space=pltpu.HBM)
    return pl.pallas_call(
        main_kernel,
        out_shape=pltpu.VMEM((N, FR, BLK, 128), BF16),
        in_specs=[hbm] * 7,
        out_specs=pl.BlockSpec(memory_space=pltpu.VMEM),
        scratch_shapes=[
            pltpu.SMEM((N,), jnp.int32),
            pltpu.VMEM((TOK, 64), BF16),
            pltpu.VMEM((2, 144, C2), BF16),
            pltpu.VMEM((1, C2), F32),
            pltpu.VMEM((1, C2), F32),
            pltpu.VMEM((1, C2), F32),
            pltpu.VMEM((HALF, 128), BF16),
            pltpu.VMEM((N, HALF, 128), BF16),
            pltpu.VMEM((C2, 304), BF16),
            pltpu.VMEM((C2, 160), BF16),
            pltpu.VMEM((C2, 128), F32),
            pltpu.VMEM((C2, 128), F32),
            pltpu.VMEM((2, 256, FL), BF16),
            pltpu.VMEM((9 * CO, 2 * C2), BF16),
            pltpu.VMEM((304, 4 * FL), BF16),
            pltpu.VMEM((2 * C2, 4 * FL), BF16),
            pltpu.VMEM((9 * CO, 4 * FL), F32),
            pltpu.VMEM((FR, TILES, CO, 128), F32),
            pltpu.VMEM((FR, N, BLK, 128), BF16),
            pltpu.SMEM((N,), jnp.int32),
            pltpu.SemaphoreType.DMA((9,)),
            pltpu.SemaphoreType.DMA((N,)),
            pltpu.SemaphoreType.DMA((N,)),
            pltpu.SemaphoreType.DMA((FR, N)),
            pltpu.SemaphoreType.DMA((FR, N)),
        ],
        compiler_params=pltpu.CompilerParams(collective_id=0, has_side_effects=True, vmem_limit_bytes=40 << 20),
    )(*(pltpu.with_memory_space_constraint(v, pltpu.HBM) for v in (strip_rows, tokens, f, b1, gain, w, b2)))


def assemble_kernel(rows_ref, recv, out):
    me = lax.axis_index("sp")

    def begin(i, start):
        return start + jnp.where(i < me, rows_ref[i], 0)

    start = lax.fori_loop(0, N, begin, 0)
    count = rows_ref[me]
    shape = (9 * 16, 256)
    p, lane = row_iota(shape), col_iota(shape)
    k, col = p // 16, p % 16
    odd = start % 2
    row = odd + k
    phase = (row % 2) * 2 + col % 2
    patch_row = row // 2
    at = phase * 32 + col // 2 + jnp.where(patch_row < 4, patch_row * PW, 128)
    pick = jnp.where((lane == at) & (k < count), 1.0, 0.0).astype(BF16)
    for f in range(FR):
        block = recv[:, f].astype(F32)
        main = block[:, :CO].reshape(C2, 128)
        tail = block[:, CO:]
        tail = jnp.concatenate([tail, pltpu.roll(tail, 128 - PW, 2), pltpu.roll(tail, 128 - 2 * PW, 2)], 1).reshape(C2, 128)
        both = jnp.concatenate([main, tail], 1).astype(BF16)
        strip = lax.dot_general(pick, both, (((1,), (1,)), ((), ())), preferred_element_type=F32)
        out[0, f] = strip.astype(BF16).reshape(9, 16, C2)


def assemble(strip_rows, recv):
    return pl.pallas_call(
        assemble_kernel,
        out_shape=jax.ShapeDtypeStruct((1, FR, 9, 16, C2), BF16),
        in_specs=[pl.BlockSpec(memory_space=pltpu.SMEM), pl.BlockSpec(memory_space=pltpu.VMEM)],
        out_specs=pl.BlockSpec(memory_space=pltpu.VMEM),
        compiler_params=pltpu.CompilerParams(vmem_limit_bytes=20 << 20),
    )(strip_rows, recv)


def per_device(tokens, strip_rows, first_filter, first_bias, norm_gain, second_filter, second_bias):
    f = first_filter.reshape(3, 9 * C, C2)
    w = jnp.transpose(second_filter, (0, 1, 2, 4, 3)).reshape(3, 9 * CO, C2)
    recv = exchange(strip_rows, tokens, f, first_bias, norm_gain, w, second_bias)
    return assemble(strip_rows, recv)


def solution(mesh):
    in_specs = (P(("req", "sp"), None), P(), P(), P(), P(), P(None, None, None, None, "sp"), P())
    out_specs = P(("req", "sp"), None, None, None, None)
    return jax.shard_map(
        per_device, mesh=mesh, in_specs=in_specs, out_specs=out_specs, check_vma=False
    )
```

```python
import jax
import jax.numpy as jnp
from jax import lax
from jax.experimental import pallas as pl
from jax.experimental.pallas import tpu as pltpu
from jax.sharding import PartitionSpec as P

C = 16
FR = 2
PH = 45
PW = 8
N = 16
TOK = FR * PH * PW // N
HALF = 24
FL = 384
LIVE = PH * PW
C2 = 384
CO = 24
TILES = 13
CHUNK = 256
MESH = pl.DeviceIdType.MESH
F32, BF16 = jnp.float32, jnp.bfloat16


def peer(i):
    return {"sp": i}


def step_of(t):
    up = (t + 1) // 2
    return 8 + up * (1 - 2 * ((t + 1) % 2))


def col_iota(shape):
    return lax.broadcasted_iota(jnp.int32, shape, len(shape) - 1)


def row_iota(shape):
    return lax.broadcasted_iota(jnp.int32, shape, len(shape) - 2)


def shift_of(phase, d):
    moved = phase + d
    return moved % 2, moved // 2


def prepare(f_ref, b1_ref, gain_ref, b2_ref, me, ft, ft0, ghalf, b2col, place, xp):
    tap1, tap2 = f_ref[0].astype(F32), f_ref[1].astype(F32)
    bias = b1_ref[...]
    hi = bias.astype(BF16).astype(F32)
    mid = (bias - hi).astype(BF16).astype(F32)
    low = bias - hi - mid
    rows = row_iota((16, C2))
    bias_rows = jnp.where(rows == 0, hi, jnp.where(rows == 1, mid, jnp.where(rows == 2, low, 0.0)))
    ft[...] = jnp.concatenate([tap2, bias_rows, tap1, jnp.zeros((80, C2), F32)], 0).T[:, :304].astype(BF16)
    ft0[...] = jnp.concatenate([bias_rows, tap2, jnp.zeros((96, C2), F32)], 0).T[:, :160].astype(BF16)
    ghalf[...] = jnp.broadcast_to(gain_ref[...] * 0.5, (128, C2)).T
    b2col[...] = jnp.broadcast_to(b2_ref[...], (128, C2)).T
    shape = (8 * HALF, FL)
    token = row_iota(shape)
    src, i = token // HALF, token % HALF
    lane = col_iota(shape)
    one, zero = jnp.ones(shape, F32), jnp.zeros(shape, F32)
    place[0] = jnp.where(lane == src * TOK + i, one, zero).astype(BF16)
    place[1] = jnp.where((lane == src * TOK + HALF + i) & (i < TOK - HALF), one, zero).astype(BF16)
    xp[144:160, :] = jnp.ones((16, 4 * FL), BF16)


def patches(f, tok_all, place, xp):
    blocks = tok_all[8 * f:8 * f + 8].astype(F32).reshape(8 * HALF, 128).T.astype(BF16)
    grid = jnp.dot(blocks[:64], place[0], preferred_element_type=F32) + jnp.dot(blocks[64:], place[1], preferred_element_type=F32)
    q = col_iota((1, FL)) % PW
    for a2 in range(2):
        for b2 in range(2):
            at = (a2 * 2 + b2) * C
            field = grid[at:at + C]
            moved = {}
            for sr in ((0, -1) if a2 == 1 else (0, 1)):
                for sq in ((0, -1) if b2 == 1 else (0, 1)):
                    piece = field
                    if sr or sq:
                        piece = pltpu.roll(piece, (-(PW * sr + sq)) % FL, 1)
                    if sq:
                        piece = jnp.where(q == (0 if sq < 0 else PW - 1), 0.0, piece)
                    moved[sr, sq] = piece.astype(BF16)
            for a in range(2):
                for b in range(2):
                    for dy in range(3):
                        for dx in range(3):
                            sa, sr = shift_of(a, dy - 1)
                            sb, sq = shift_of(b, dx - 1)
                            if (sa, sb) == (a2, b2):
                                row = (160 if f == 0 else 0) + (dy * 3 + dx) * C
                                ph = a * 2 + b
                                xp[row:row + C, ph * FL:(ph + 1) * FL] = moved[sr, sq]


def convolve(f, xp, ft, ft0, ghalf, wcat, hid, prod):
    def first_of(at):
        lanes = slice(at, at + CHUNK)
        if f == 0:
            return jnp.dot(ft0[...], xp[144:304, lanes], preferred_element_type=F32)
        return jnp.dot(ft[...], xp[:, lanes], preferred_element_type=F32)

    def second_of(at):
        lanes = slice(at, at + CHUNK)
        if f == 0:
            prod[:, lanes] = jnp.dot(wcat[:, C2:], hid[0:C2, lanes], preferred_element_type=F32)
        else:
            prod[:, lanes] = jnp.dot(wcat[...], hid[:, lanes], preferred_element_type=F32)

    def act(at, first):
        lanes = slice(at, at + CHUNK)
        mean = jnp.sum(first * first, axis=0, keepdims=True) * (1.0 / C2)
        live = (col_iota((1, CHUNK)) + at) % FL < LIVE
        scale = jnp.where(live, lax.rsqrt(mean + 1e-6), 0.0)
        gain = jnp.concatenate([ghalf[...]] * (CHUNK // 128), 1)
        u = first * scale * gain
        hid[f * C2:(f + 1) * C2, lanes] = (u + u * jnp.tanh(u)).astype(BF16)

    ats = list(range(0, 4 * FL, CHUNK))
    ready = first_of(ats[0])
    for n, at in enumerate(ats):
        ahead = first_of(ats[n + 1]) if n + 1 < len(ats) else None
        act(at, ready)
        if n:
            second_of(ats[n - 1])
        ready = ahead
    second_of(ats[-1])


def gather_taps(f, me, prod, b2col, fin, rot):
    q = col_iota((1, FL)) % PW
    bias = b2col[pl.ds(pl.multiple_of(me * CO, 8), CO), :]
    bias = jnp.concatenate([bias] * (FL // 128), 1)
    outs = []
    for a in range(2):
        for b in range(2):
            sums = {}
            for dy in range(3):
                for dx in range(3):
                    sa, sr = shift_of(a, dy - 1)
                    sb, sq = shift_of(b, dx - 1)
                    tap, ph = dy * 3 + dx, sa * 2 + sb
                    term = prod[tap * CO:(tap + 1) * CO, ph * FL:(ph + 1) * FL]
                    sums[sr, sq] = sums[sr, sq] + term if (sr, sq) in sums else term
            sr, sq = (-1, 1)[a], (-1, 1)[b]
            side = sums[0, sq] + pltpu.roll(sums[sr, sq], (-PW * sr) % FL, 1)
            side = pltpu.roll(side, (-sq) % FL, 1)
            side = jnp.where(q == (0 if sq < 0 else PW - 1), 0.0, side)
            outs.append(sums[0, 0] + pltpu.roll(sums[sr, 0], (-PW * sr) % FL, 1) + side + bias)
    block = col_iota((1, 128)) // 32
    for t in range(FL // 128):
        for j in range(4):
            tile = None
            for ph in range(4):
                piece = outs[ph][:, 128 * t:128 * t + 128]
                if ph != j:
                    piece = pltpu.roll(piece, (32 * (ph - j)) % 128, 1)
                tile = piece if tile is None else jnp.where(block == ph, piece, tile)
            fin[f, 4 * t + j] = tile
            parts = [tile[8 * m:8 * m + 8] for m in range(3)]
            parts = [pltpu.roll(v, 8 * m + 64 * f, 1) if m or f else v for m, v in enumerate(parts)]
            rot[f, 4 * t + j] = jnp.concatenate(parts, 0)
    fin[f, TILES - 1] = jnp.zeros((CO, 128), F32)
    rot[f, TILES - 1] = jnp.zeros((CO, 128), F32)


def cut_strips(f, starts, fin, rot, send):
    lane = col_iota((1, 128))
    row = (lane % 32) // PW * 2 + lane // 64
    for to in range(N):
        start = starts[to]
        tile, off = start // 8, start % 8
        main = jnp.where(row >= off, fin[f, tile], fin[f, tile + 1])
        if f == 0:
            send[to] = main.astype(BF16)
            continue
        slot = (lane // 8 + 16 - (off % 2 * 8 + off // 2)) % 16
        tail = None
        for g in range(FR):
            ninth = rot[g, tile + 1]
            for m in range(3):
                part = ninth[8 * m:8 * m + 8]
                tail = part if tail is None else jnp.where((slot // 8 == g) & (slot % 4 == m), part, tail)
        send[to] = jnp.concatenate([main, tail], 0).astype(BF16)


def main_kernel(
    rows_ref, tok_ref, f_ref, b1_ref, gain_ref, w_ref, b2_ref, recv0, recv1,
    rows, tokv, fv, b1v, gainv, b2v, pack, tok_all, ft, ft0, ghalf, b2col, place, wcat, xp, hid, prod, fin, rot, send0, send1,
    starts, local_sem, tok_send, tok_recv, out_send, out_recv,
):
    me = lax.axis_index("sp")
    barrier = pltpu.get_barrier_semaphore()

    def greet(i, carry):
        pl.semaphore_signal(barrier, inc=1, device_id=peer(lax.rem(me + i, N)), device_id_type=MESH)
        return carry

    lax.fori_loop(1, N, greet, 0)

    copies = [
        (tok_ref, tokv), (f_ref.at[1], fv.at[0]), (f_ref.at[2], fv.at[1]), (b1_ref, b1v.at[0]), (gain_ref, gainv.at[0]), (b2_ref, b2v.at[0]),
        (w_ref.at[1], wcat.at[:, 0:C2]), (w_ref.at[2], wcat.at[:, C2:2 * C2]), (rows_ref, rows),
    ]
    copies = [pltpu.make_async_copy(s, d, local_sem.at[i]) for i, (s, d) in enumerate(copies)]
    for copy in copies:
        copy.start()

    copies[0].wait()
    tokens = tokv[...].astype(F32)
    right = jnp.concatenate([tokens[HALF:], jnp.zeros((2 * HALF - TOK, 64), F32)], 0)
    block = jnp.concatenate([tokens[:HALF], right], 1).astype(BF16)
    pack[...] = block
    tok_all[me] = block
    pl.semaphore_wait(barrier, N - 1)

    def tok_copy(to):
        return pltpu.make_async_remote_copy(
            src_ref=pack, dst_ref=tok_all.at[me], send_sem=tok_send, recv_sem=tok_recv.at[me // 8],
            device_id=peer(to), device_id_type=MESH,
        )

    def tok_start(t, carry):
        tok_copy(lax.rem(me + step_of(t), N)).start()
        return carry

    lax.fori_loop(0, N - 1, tok_start, 0)

    for copy in copies[1:]:
        copy.wait()

    def begin(i, start):
        starts[i] = start
        return start + rows[i]

    lax.fori_loop(0, N, begin, 0)
    prepare(fv, b1v, gainv, b2v, me, ft, ft0, ghalf, b2col, place, xp)

    after = lax.rem(me + 1, N)

    def tok_wait(f, count):
        slabs = tok_all.at[pl.ds(0, count)]
        pltpu.make_async_remote_copy(
            src_ref=slabs, dst_ref=slabs, send_sem=tok_send, recv_sem=tok_recv.at[f], device_id=peer(after), device_id_type=MESH
        ).wait_recv()

    def out_copy(f, source, target, to):
        return pltpu.make_async_remote_copy(
            src_ref=source, dst_ref=target, send_sem=out_send.at[f], recv_sem=out_recv.at[f],
            device_id=peer(to), device_id_type=MESH,
        )

    for f, (send, recv) in enumerate(((send0, recv0), (send1, recv1))):
        @pl.when(me // 8 == f)
        def _():
            tok_wait(f, 7)

        @pl.when(me // 8 != f)
        def _():
            tok_wait(f, 8)

        patches(f, tok_all, place, xp)
        convolve(f, xp, ft, ft0, ghalf, wcat, hid, prod)
        gather_taps(f, me, prod, b2col, fin, rot)
        cut_strips(f, starts, fin, rot, send)

        def out_start(t, carry):
            to = lax.rem(me + step_of(t), N)
            out_copy(f, send.at[to], recv.at[me], to).start()
            return carry

        lax.fori_loop(0, N - 1, out_start, 0)
        recv[me] = send[me]

    pltpu.make_async_remote_copy(
        src_ref=tok_all.at[pl.ds(0, N - 1)], dst_ref=tok_all.at[pl.ds(0, N - 1)], send_sem=tok_send, recv_sem=tok_recv.at[0],
        device_id=peer(after), device_id_type=MESH,
    ).wait_send()
    for f, (send, recv) in enumerate(((send0, recv0), (send1, recv1))):
        out_copy(f, send.at[pl.ds(0, N - 1)], recv.at[pl.ds(0, N - 1)], after).wait()


def exchange(strip_rows, tokens, f, b1, gain, w, b2):
    hbm = pl.BlockSpec(memory_space=pltpu.HBM)
    return pl.pallas_call(
        main_kernel,
        out_shape=(pltpu.VMEM((N, CO, 128), BF16), pltpu.VMEM((N, CO + 8, 128), BF16)),
        in_specs=[hbm] * 7,
        out_specs=(pl.BlockSpec(memory_space=pltpu.VMEM),) * 2,
        scratch_shapes=[
            pltpu.SMEM((N,), jnp.int32),
            pltpu.VMEM((TOK, 64), BF16),
            pltpu.VMEM((2, 144, C2), BF16),
            pltpu.VMEM((1, C2), F32),
            pltpu.VMEM((1, C2), F32),
            pltpu.VMEM((1, C2), F32),
            pltpu.VMEM((HALF, 128), BF16),
            pltpu.VMEM((N, HALF, 128), BF16),
            pltpu.VMEM((C2, 304), BF16),
            pltpu.VMEM((C2, 160), BF16),
            pltpu.VMEM((C2, 128), F32),
            pltpu.VMEM((C2, 128), F32),
            pltpu.VMEM((2, 8 * HALF, FL), BF16),
            pltpu.VMEM((9 * CO, 2 * C2), BF16),
            pltpu.VMEM((304, 4 * FL), BF16),
            pltpu.VMEM((2 * C2, 4 * FL), BF16),
            pltpu.VMEM((9 * CO, 4 * FL), F32),
            pltpu.VMEM((FR, TILES, CO, 128), F32),
            pltpu.VMEM((FR, TILES, CO, 128), F32),
            pltpu.VMEM((N, CO, 128), BF16),
            pltpu.VMEM((N, CO + 8, 128), BF16),
            pltpu.SMEM((N,), jnp.int32),
            pltpu.SemaphoreType.DMA((9,)),
            pltpu.SemaphoreType.DMA,
            pltpu.SemaphoreType.DMA((FR,)),
            pltpu.SemaphoreType.DMA((FR,)),
            pltpu.SemaphoreType.DMA((FR,)),
        ],
        compiler_params=pltpu.CompilerParams(collective_id=0, has_side_effects=True, vmem_limit_bytes=40 << 20),
    )(*(pltpu.with_memory_space_constraint(v, pltpu.HBM) for v in (strip_rows, tokens, f, b1, gain, w, b2)))


def assemble_kernel(rows_ref, recv0, recv1, out):
    me = lax.axis_index("sp")

    def begin(i, start):
        return start + jnp.where(i < me, rows_ref[i], 0)

    start = lax.fori_loop(0, N, begin, 0)
    count = rows_ref[me]
    shape = (9 * 16, 256)
    p, lane = row_iota(shape), col_iota(shape)
    k, col = p // 16, p % 16
    row = (start + k) % 8
    at = row % 2 * 64 + col % 2 * 32 + row // 2 * PW + col // 2 + jnp.where(k == 8, 128, 0)
    pick = jnp.where((lane == at) & (k < count), 1.0, 0.0).astype(BF16)
    tail = recv1[...].astype(F32)[:, CO:]
    for f, recv in enumerate((recv0, recv1)):
        main = recv[...].astype(F32)[:, :CO].reshape(C2, 128)
        turns = [8 * m + 64 * f for m in range(3)]
        ninth = jnp.concatenate([pltpu.roll(tail, 128 - n, 2) if n else tail for n in turns], 1).reshape(C2, 128)
        both = jnp.concatenate([main, ninth], 1).astype(BF16)
        strip = lax.dot_general(pick, both, (((1,), (1,)), ((), ())), preferred_element_type=F32)
        out[0, f] = strip.astype(BF16).reshape(9, 16, C2)


def assemble(strip_rows, recv0, recv1):
    vmem = pl.BlockSpec(memory_space=pltpu.VMEM)
    return pl.pallas_call(
        assemble_kernel,
        out_shape=jax.ShapeDtypeStruct((1, FR, 9, 16, C2), BF16),
        in_specs=[pl.BlockSpec(memory_space=pltpu.SMEM), vmem, vmem],
        out_specs=vmem,
        compiler_params=pltpu.CompilerParams(vmem_limit_bytes=20 << 20),
    )(strip_rows, recv0, recv1)


def per_device(tokens, strip_rows, first_filter, first_bias, norm_gain, second_filter, second_bias):
    f = first_filter.reshape(3, 9 * C, C2)
    w = jnp.transpose(second_filter, (0, 1, 2, 4, 3)).reshape(3, 9 * CO, C2)
    recv0, recv1 = exchange(strip_rows, tokens, f, first_bias, norm_gain, w, second_bias)
    return assemble(strip_rows, recv0, recv1)


def solution(mesh):
    in_specs = (P(("req", "sp"), None), P(), P(), P(), P(), P(None, None, None, None, "sp"), P())
    out_specs = P(("req", "sp"), None, None, None, None)
    return jax.shard_map(
        per_device, mesh=mesh, in_specs=in_specs, out_specs=out_specs, check_vma=False
    )
```

```python
import jax
import jax.numpy as jnp
from jax import lax
from jax.experimental import pallas as pl
from jax.experimental.pallas import tpu as pltpu
from jax.sharding import PartitionSpec as P

C = 16
FR = 2
PH = 45
PW = 8
N = 16
NF = N // FR
TOK = FR * PH * PW // N
HALF = 24
FL = 384
LIVE = PH * PW
C2 = 384
CO = 24
TILES = 13
CHUNK = 256
MESH = pl.DeviceIdType.MESH
F32, BF16 = jnp.float32, jnp.bfloat16


def peer(i):
    return {"sp": i}


def for_others(me, low, high, act):
    def step(i, carry):
        @pl.when(i != me)
        def _():
            act(i)

        return carry

    lax.fori_loop(low, high, step, 0)


def col_iota(shape):
    return lax.broadcasted_iota(jnp.int32, shape, len(shape) - 1)


def row_iota(shape):
    return lax.broadcasted_iota(jnp.int32, shape, len(shape) - 2)


def shift_of(phase, d):
    moved = phase + d
    return moved % 2, moved // 2


def prepare(f_ref, b1_ref, gain_ref, b2_ref, me, ft, ft0, ghalf, b2col, place, xp):
    tap1, tap2 = f_ref[0].astype(F32), f_ref[1].astype(F32)
    bias = b1_ref[...]
    hi = bias.astype(BF16).astype(F32)
    mid = (bias - hi).astype(BF16).astype(F32)
    low = bias - hi - mid
    rows = row_iota((16, C2))
    bias_rows = jnp.where(rows == 0, hi, jnp.where(rows == 1, mid, jnp.where(rows == 2, low, 0.0)))
    ft[...] = jnp.concatenate([tap2, bias_rows, tap1, jnp.zeros((80, C2), F32)], 0).T[:, :304].astype(BF16)
    ft0[...] = jnp.concatenate([bias_rows, tap2, jnp.zeros((96, C2), F32)], 0).T[:, :160].astype(BF16)
    ghalf[...] = jnp.broadcast_to(gain_ref[...] * 0.5, (128, C2)).T
    b2col[...] = jnp.broadcast_to(b2_ref[...], (128, C2)).T
    shape = (8 * HALF, FL)
    token = row_iota(shape)
    src, i = token // HALF, token % HALF
    lane = col_iota(shape)
    one, zero = jnp.ones(shape, F32), jnp.zeros(shape, F32)
    place[0] = jnp.where(lane == src * TOK + i, one, zero).astype(BF16)
    place[1] = jnp.where((lane == src * TOK + HALF + i) & (i < TOK - HALF), one, zero).astype(BF16)
    xp[144:160, :] = jnp.ones((16, 4 * FL), BF16)


def patches(f, tok_all, place, xp):
    blocks = tok_all[8 * f:8 * f + 8].astype(F32).reshape(8 * HALF, 128).T.astype(BF16)
    grid = jnp.dot(blocks[:64], place[0], preferred_element_type=F32) + jnp.dot(blocks[64:], place[1], preferred_element_type=F32)
    q = col_iota((1, FL)) % PW
    for a2 in range(2):
        for b2 in range(2):
            at = (a2 * 2 + b2) * C
            field = grid[at:at + C]
            moved = {}
            for sr in ((0, -1) if a2 == 1 else (0, 1)):
                for sq in ((0, -1) if b2 == 1 else (0, 1)):
                    piece = field
                    if sr or sq:
                        piece = pltpu.roll(piece, (-(PW * sr + sq)) % FL, 1)
                    if sq:
                        piece = jnp.where(q == (0 if sq < 0 else PW - 1), 0.0, piece)
                    moved[sr, sq] = piece.astype(BF16)
            for a in range(2):
                for b in range(2):
                    for dy in range(3):
                        for dx in range(3):
                            sa, sr = shift_of(a, dy - 1)
                            sb, sq = shift_of(b, dx - 1)
                            if (sa, sb) == (a2, b2):
                                row = (160 if f == 0 else 0) + (dy * 3 + dx) * C
                                ph = a * 2 + b
                                xp[row:row + C, ph * FL:(ph + 1) * FL] = moved[sr, sq]


def convolve(f, xp, ft, ft0, ghalf, wcat, hid, prod):
    def first_of(at):
        lanes = slice(at, at + CHUNK)
        if f == 0:
            return jnp.dot(ft0[...], xp[144:304, lanes], preferred_element_type=F32)
        return jnp.dot(ft[...], xp[:, lanes], preferred_element_type=F32)

    def second_of(at):
        lanes = slice(at, at + CHUNK)
        if f == 0:
            prod[:, lanes] = jnp.dot(wcat[:, C2:], hid[0:C2, lanes], preferred_element_type=F32)
        else:
            prod[:, lanes] = jnp.dot(wcat[...], hid[:, lanes], preferred_element_type=F32)

    def act(at, first):
        lanes = slice(at, at + CHUNK)
        mean = jnp.sum(first * first, axis=0, keepdims=True) * (1.0 / C2)
        live = (col_iota((1, CHUNK)) + at) % FL < LIVE
        scale = jnp.where(live, lax.rsqrt(mean + 1e-6), 0.0)
        gain = jnp.concatenate([ghalf[...]] * (CHUNK // 128), 1)
        u = first * scale * gain
        hid[f * C2:(f + 1) * C2, lanes] = (u + u * jnp.tanh(u)).astype(BF16)

    ats = list(range(0, 4 * FL, CHUNK))
    ready = first_of(ats[0])
    for n, at in enumerate(ats):
        ahead = first_of(ats[n + 1]) if n + 1 < len(ats) else None
        act(at, ready)
        if n:
            second_of(ats[n - 1])
        ready = ahead
    second_of(ats[-1])


def gather_taps(f, me, prod, b2col, fin, rot):
    q = col_iota((1, FL)) % PW
    bias = b2col[pl.ds(pl.multiple_of(me * CO, 8), CO), :]
    bias = jnp.concatenate([bias] * (FL // 128), 1)
    outs = []
    for a in range(2):
        for b in range(2):
            sums = {}
            for dy in range(3):
                for dx in range(3):
                    sa, sr = shift_of(a, dy - 1)
                    sb, sq = shift_of(b, dx - 1)
                    tap, ph = dy * 3 + dx, sa * 2 + sb
                    term = prod[tap * CO:(tap + 1) * CO, ph * FL:(ph + 1) * FL]
                    sums[sr, sq] = sums[sr, sq] + term if (sr, sq) in sums else term
            sr, sq = (-1, 1)[a], (-1, 1)[b]
            side = sums[0, sq] + pltpu.roll(sums[sr, sq], (-PW * sr) % FL, 1)
            side = pltpu.roll(side, (-sq) % FL, 1)
            side = jnp.where(q == (0 if sq < 0 else PW - 1), 0.0, side)
            outs.append(sums[0, 0] + pltpu.roll(sums[sr, 0], (-PW * sr) % FL, 1) + side + bias)
    block = col_iota((1, 128)) // 32
    for t in range(FL // 128):
        for j in range(4):
            tile = None
            for ph in range(4):
                piece = outs[ph][:, 128 * t:128 * t + 128]
                if ph != j:
                    piece = pltpu.roll(piece, (32 * (ph - j)) % 128, 1)
                tile = piece if tile is None else jnp.where(block == ph, piece, tile)
            fin[f, 4 * t + j] = tile
            parts = [tile[8 * m:8 * m + 8] for m in range(3)]
            parts = [pltpu.roll(v, 8 * m + 64 * f, 1) if m or f else v for m, v in enumerate(parts)]
            rot[f, 4 * t + j] = jnp.concatenate(parts, 0)
    fin[f, TILES - 1] = jnp.zeros((CO, 128), F32)
    rot[f, TILES - 1] = jnp.zeros((CO, 128), F32)


def cut_strips(f, starts, fin, rot, send):
    lane = col_iota((1, 128))
    row = (lane % 32) // PW * 2 + lane // 64
    for to in range(N):
        start = starts[to]
        tile, off = start // 8, start % 8
        main = jnp.where(row >= off, fin[f, tile], fin[f, tile + 1])
        if f == 0:
            send[to] = main.astype(BF16)
            continue
        slot = (lane // 8 + 16 - (off % 2 * 8 + off // 2)) % 16
        tail = None
        for g in range(FR):
            ninth = rot[g, tile + 1]
            for m in range(3):
                part = ninth[8 * m:8 * m + 8]
                tail = part if tail is None else jnp.where((slot // 8 == g) & (slot % 4 == m), part, tail)
        send[to] = jnp.concatenate([main, tail], 0).astype(BF16)


def strip_pick(start, count):
    shape = (9 * 16, 256)
    p, lane = row_iota(shape), col_iota(shape)
    k, col = p // 16, p % 16
    row = (start + k) % 8
    at = row % 2 * 64 + col % 2 * 32 + row // 2 * PW + col // 2 + jnp.where(k == 8, 128, 0)
    return jnp.where((lane == at) & (k < count), 1.0, 0.0).astype(BF16)


def main_kernel(
    rows_ref, tok_ref, f_ref, b1_ref, gain_ref, w_ref, b2_ref, recv0, recv1, pick,
    rows, tokv, fv, b1v, gainv, b2v, pack, tok_all, ft, ft0, ghalf, b2col, place, wcat, xp, hid, prod, fin, rot, send0, send1,
    starts, local_sem, go, tok_send, tok_recv, out_send, out_recv,
):
    me = lax.axis_index("sp")
    early = me < NF
    barrier = pltpu.get_barrier_semaphore()

    def greet(i):
        pl.semaphore_signal(barrier, inc=1, device_id=peer(i), device_id_type=MESH)

    def tok_copy(to):
        return pltpu.make_async_remote_copy(
            src_ref=pack, dst_ref=tok_all.at[me], send_sem=tok_send, recv_sem=tok_recv.at[me // NF],
            device_id=peer(to), device_id_type=MESH,
        )

    @pl.when(early)
    def _():
        for_others(me, 0, NF, greet)

    @pl.when(jnp.logical_not(early))
    def _():
        pl.semaphore_wait(barrier, NF)
        for_others(me, 0, NF, greet)

    copies = [
        (tok_ref, tokv), (f_ref.at[1], fv.at[0]), (f_ref.at[2], fv.at[1]), (b1_ref, b1v.at[0]), (gain_ref, gainv.at[0]), (b2_ref, b2v.at[0]),
        (w_ref.at[1], wcat.at[:, 0:C2]), (w_ref.at[2], wcat.at[:, C2:2 * C2]), (rows_ref, rows),
    ]
    copies = [pltpu.make_async_copy(s, d, local_sem.at[i]) for i, (s, d) in enumerate(copies)]
    for copy in copies:
        copy.start()

    copies[0].wait()
    tokens = tokv[...].astype(F32)
    right = jnp.concatenate([tokens[HALF:], jnp.zeros((2 * HALF - TOK, 64), F32)], 0)
    block = jnp.concatenate([tokens[:HALF], right], 1).astype(BF16)
    pack[...] = block
    tok_all[me] = block

    @pl.when(early)
    def _():
        pl.semaphore_wait(barrier, NF - 1)
        for_others(me, NF, N, greet)

    for_others(me, 0, NF, lambda i: tok_copy(i).start())

    for copy in copies[1:]:
        copy.wait()

    def begin(i, start):
        starts[i] = start
        return start + rows[i]

    lax.fori_loop(0, N, begin, 0)
    prepare(fv, b1v, gainv, b2v, me, ft, ft0, ghalf, b2col, place, xp)
    pick[...] = strip_pick(starts[me], rows[me])

    @pl.when(early)
    def _():
        pl.semaphore_wait(barrier, NF)
        pl.semaphore_signal(go, inc=1, device_id=peer(me + NF), device_id_type=MESH)

    @pl.when(jnp.logical_not(early))
    def _():
        pl.semaphore_wait(go, 1)

    for_others(me, NF, N, lambda i: tok_copy(i).start())

    after = lax.rem(me + 1, N)

    def tok_wait(f, count):
        slabs = tok_all.at[pl.ds(0, count)]
        pltpu.make_async_remote_copy(
            src_ref=slabs, dst_ref=slabs, send_sem=tok_send, recv_sem=tok_recv.at[f], device_id=peer(after), device_id_type=MESH
        ).wait_recv()

    def out_copy(f, source, target, to):
        return pltpu.make_async_remote_copy(
            src_ref=source, dst_ref=target, send_sem=out_send.at[f], recv_sem=out_recv.at[f],
            device_id=peer(to), device_id_type=MESH,
        )

    for f, (send, recv) in enumerate(((send0, recv0), (send1, recv1))):
        @pl.when(me // NF == f)
        def _():
            tok_wait(f, NF - 1)

        @pl.when(me // NF != f)
        def _():
            tok_wait(f, NF)

        patches(f, tok_all, place, xp)
        convolve(f, xp, ft, ft0, ghalf, wcat, hid, prod)
        gather_taps(f, me, prod, b2col, fin, rot)
        cut_strips(f, starts, fin, rot, send)

        for_others(me, 0, N, lambda to: out_copy(f, send.at[to], recv.at[me], to).start())
        recv[me] = send[me]

    pltpu.make_async_remote_copy(
        src_ref=tok_all.at[pl.ds(0, N - 1)], dst_ref=tok_all.at[pl.ds(0, N - 1)], send_sem=tok_send, recv_sem=tok_recv.at[0],
        device_id=peer(after), device_id_type=MESH,
    ).wait_send()
    for f, (send, recv) in enumerate(((send0, recv0), (send1, recv1))):
        out_copy(f, send.at[pl.ds(0, N - 1)], recv.at[pl.ds(0, N - 1)], after).wait()


def exchange(strip_rows, tokens, f, b1, gain, w, b2):
    hbm = pl.BlockSpec(memory_space=pltpu.HBM)
    return pl.pallas_call(
        main_kernel,
        out_shape=(pltpu.VMEM((N, CO, 128), BF16), pltpu.VMEM((N, CO + 8, 128), BF16), pltpu.VMEM((9 * 16, 256), BF16)),
        in_specs=[hbm] * 7,
        out_specs=(pl.BlockSpec(memory_space=pltpu.VMEM),) * 3,
        scratch_shapes=[
            pltpu.SMEM((N,), jnp.int32),
            pltpu.VMEM((TOK, 64), BF16),
            pltpu.VMEM((2, 144, C2), BF16),
            pltpu.VMEM((1, C2), F32),
            pltpu.VMEM((1, C2), F32),
            pltpu.VMEM((1, C2), F32),
            pltpu.VMEM((HALF, 128), BF16),
            pltpu.VMEM((N, HALF, 128), BF16),
            pltpu.VMEM((C2, 304), BF16),
            pltpu.VMEM((C2, 160), BF16),
            pltpu.VMEM((C2, 128), F32),
            pltpu.VMEM((C2, 128), F32),
            pltpu.VMEM((2, 8 * HALF, FL), BF16),
            pltpu.VMEM((9 * CO, 2 * C2), BF16),
            pltpu.VMEM((304, 4 * FL), BF16),
            pltpu.VMEM((2 * C2, 4 * FL), BF16),
            pltpu.VMEM((9 * CO, 4 * FL), F32),
            pltpu.VMEM((FR, TILES, CO, 128), F32),
            pltpu.VMEM((FR, TILES, CO, 128), F32),
            pltpu.VMEM((N, CO, 128), BF16),
            pltpu.VMEM((N, CO + 8, 128), BF16),
            pltpu.SMEM((N,), jnp.int32),
            pltpu.SemaphoreType.DMA((9,)),
            pltpu.SemaphoreType.REGULAR,
            pltpu.SemaphoreType.DMA,
            pltpu.SemaphoreType.DMA((FR,)),
            pltpu.SemaphoreType.DMA((FR,)),
            pltpu.SemaphoreType.DMA((FR,)),
        ],
        compiler_params=pltpu.CompilerParams(collective_id=0, has_side_effects=True, vmem_limit_bytes=40 << 20),
    )(*(pltpu.with_memory_space_constraint(v, pltpu.HBM) for v in (strip_rows, tokens, f, b1, gain, w, b2)))


def assemble_kernel(pick, recv0, recv1, out):
    tail = recv1[...].astype(F32)[:, CO:]
    for f, recv in enumerate((recv0, recv1)):
        main = recv[...].astype(F32)[:, :CO].reshape(C2, 128)
        turns = [8 * m + 64 * f for m in range(3)]
        ninth = jnp.concatenate([pltpu.roll(tail, 128 - n, 2) if n else tail for n in turns], 1).reshape(C2, 128)
        both = jnp.concatenate([main, ninth], 1).astype(BF16)
        strip = lax.dot_general(pick[...], both, (((1,), (1,)), ((), ())), preferred_element_type=F32)
        out[0, f] = strip.astype(BF16).reshape(9, 16, C2)


def assemble(pick, recv0, recv1):
    vmem = pl.BlockSpec(memory_space=pltpu.VMEM)
    return pl.pallas_call(
        assemble_kernel,
        out_shape=jax.ShapeDtypeStruct((1, FR, 9, 16, C2), BF16),
        in_specs=[vmem] * 3,
        out_specs=vmem,
        compiler_params=pltpu.CompilerParams(vmem_limit_bytes=20 << 20),
    )(pick, recv0, recv1)


def per_device(tokens, strip_rows, first_filter, first_bias, norm_gain, second_filter, second_bias):
    f = first_filter.reshape(3, 9 * C, C2)
    w = jnp.transpose(second_filter, (0, 1, 2, 4, 3)).reshape(3, 9 * CO, C2)
    recv0, recv1, pick = exchange(strip_rows, tokens, f, first_bias, norm_gain, w, second_bias)
    return assemble(pick, recv0, recv1)


def solution(mesh):
    in_specs = (P(("req", "sp"), None), P(), P(), P(), P(), P(None, None, None, None, "sp"), P())
    out_specs = P(("req", "sp"), None, None, None, None)
    return jax.shard_map(
        per_device, mesh=mesh, in_specs=in_specs, out_specs=out_specs, check_vma=False
    )
```

```python
import jax
import jax.numpy as jnp
from jax import lax
from jax.experimental import pallas as pl
from jax.experimental.pallas import tpu as pltpu
from jax.sharding import PartitionSpec as P

C = 16
FR = 2
PH = 45
PW = 8
N = 16
NF = N // FR
TOK = FR * PH * PW // N
HALF = 24
FL = 384
LIVE = PH * PW
C2 = 384
CO = 24
TILES = 13
CHUNK = 256
MESH = pl.DeviceIdType.MESH
F32, BF16 = jnp.float32, jnp.bfloat16


def peer(i):
    return {"sp": i}


def for_others(me, low, high, act):
    def step(i, carry):
        @pl.when(i != me)
        def _():
            act(i)

        return carry

    lax.fori_loop(low, high, step, 0)


def col_iota(shape):
    return lax.broadcasted_iota(jnp.int32, shape, len(shape) - 1)


def row_iota(shape):
    return lax.broadcasted_iota(jnp.int32, shape, len(shape) - 2)


def shift_of(phase, d):
    moved = phase + d
    return moved % 2, moved // 2


def prepare(f_ref, b1_ref, gain_ref, b2_ref, me, ft, ft0, ghalf, b2col, place, xp):
    tap1, tap2 = f_ref[0].astype(F32), f_ref[1].astype(F32)
    bias = b1_ref[...]
    hi = bias.astype(BF16).astype(F32)
    mid = (bias - hi).astype(BF16).astype(F32)
    low = bias - hi - mid
    rows = row_iota((16, C2))
    bias_rows = jnp.where(rows == 0, hi, jnp.where(rows == 1, mid, jnp.where(rows == 2, low, 0.0)))
    ft[...] = jnp.concatenate([tap2, bias_rows, tap1, jnp.zeros((80, C2), F32)], 0).T[:, :304].astype(BF16)
    ft0[...] = jnp.concatenate([bias_rows, tap2, jnp.zeros((96, C2), F32)], 0).T[:, :160].astype(BF16)
    ghalf[...] = jnp.broadcast_to(gain_ref[...] * 0.5, (128, C2)).T
    b2col[...] = jnp.broadcast_to(b2_ref[...], (128, C2)).T
    shape = (8 * HALF, FL)
    token = row_iota(shape)
    src, i = token // HALF, token % HALF
    lane = col_iota(shape)
    one, zero = jnp.ones(shape, F32), jnp.zeros(shape, F32)
    place[0] = jnp.where(lane == src * TOK + i, one, zero).astype(BF16)
    place[1] = jnp.where((lane == src * TOK + HALF + i) & (i < TOK - HALF), one, zero).astype(BF16)
    xp[144:160, :] = jnp.ones((16, 4 * FL), BF16)


def patches(f, tok_all, place, xp):
    blocks = tok_all[8 * f:8 * f + 8].astype(F32).reshape(8 * HALF, 128).T.astype(BF16)
    grid = jnp.dot(blocks[:64], place[0], preferred_element_type=F32) + jnp.dot(blocks[64:], place[1], preferred_element_type=F32)
    q = col_iota((1, FL)) % PW
    for a2 in range(2):
        for b2 in range(2):
            at = (a2 * 2 + b2) * C
            field = grid[at:at + C]
            moved = {}
            for sr in ((0, -1) if a2 == 1 else (0, 1)):
                for sq in ((0, -1) if b2 == 1 else (0, 1)):
                    piece = field
                    if sr or sq:
                        piece = pltpu.roll(piece, (-(PW * sr + sq)) % FL, 1)
                    if sq:
                        piece = jnp.where(q == (0 if sq < 0 else PW - 1), 0.0, piece)
                    moved[sr, sq] = piece.astype(BF16)
            for a in range(2):
                for b in range(2):
                    for dy in range(3):
                        for dx in range(3):
                            sa, sr = shift_of(a, dy - 1)
                            sb, sq = shift_of(b, dx - 1)
                            if (sa, sb) == (a2, b2):
                                row = (160 if f == 0 else 0) + (dy * 3 + dx) * C
                                ph = a * 2 + b
                                xp[row:row + C, ph * FL:(ph + 1) * FL] = moved[sr, sq]


def convolve(f, xp, ft, ft0, ghalf, wcat, hid, prod):
    def first_of(at):
        lanes = slice(at, at + CHUNK)
        if f == 0:
            return jnp.dot(ft0[...], xp[144:304, lanes], preferred_element_type=F32)
        return jnp.dot(ft[...], xp[:, lanes], preferred_element_type=F32)

    def second_of(at):
        lanes = slice(at, at + CHUNK)
        if f == 0:
            prod[:, lanes] = jnp.dot(wcat[:, C2:], hid[0:C2, lanes], preferred_element_type=F32)
        else:
            prod[:, lanes] = jnp.dot(wcat[...], hid[:, lanes], preferred_element_type=F32)

    def act(at, first):
        lanes = slice(at, at + CHUNK)
        mean = jnp.sum(first * first, axis=0, keepdims=True) * (1.0 / C2)
        live = (col_iota((1, CHUNK)) + at) % FL < LIVE
        scale = jnp.where(live, lax.rsqrt(mean + 1e-6), 0.0)
        gain = jnp.concatenate([ghalf[...]] * (CHUNK // 128), 1)
        u = first * scale * gain
        hid[f * C2:(f + 1) * C2, lanes] = (u + u * jnp.tanh(u)).astype(BF16)

    ats = list(range(0, 4 * FL, CHUNK))
    ready = first_of(ats[0])
    for n, at in enumerate(ats):
        ahead = first_of(ats[n + 1]) if n + 1 < len(ats) else None
        act(at, ready)
        if n:
            second_of(ats[n - 1])
        ready = ahead
    second_of(ats[-1])


def gather_taps(f, me, prod, b2col, fin, rot):
    q = col_iota((1, FL)) % PW
    bias = b2col[pl.ds(pl.multiple_of(me * CO, 8), CO), :]
    bias = jnp.concatenate([bias] * (FL // 128), 1)
    outs = []
    for a in range(2):
        for b in range(2):
            sums = {}
            for dy in range(3):
                for dx in range(3):
                    sa, sr = shift_of(a, dy - 1)
                    sb, sq = shift_of(b, dx - 1)
                    tap, ph = dy * 3 + dx, sa * 2 + sb
                    term = prod[tap * CO:(tap + 1) * CO, ph * FL:(ph + 1) * FL]
                    sums[sr, sq] = sums[sr, sq] + term if (sr, sq) in sums else term
            sr, sq = (-1, 1)[a], (-1, 1)[b]
            side = sums[0, sq] + pltpu.roll(sums[sr, sq], (-PW * sr) % FL, 1)
            side = pltpu.roll(side, (-sq) % FL, 1)
            side = jnp.where(q == (0 if sq < 0 else PW - 1), 0.0, side)
            outs.append(sums[0, 0] + pltpu.roll(sums[sr, 0], (-PW * sr) % FL, 1) + side + bias)
    block = col_iota((1, 128)) // 32
    for t in range(FL // 128):
        for j in range(4):
            tile = None
            for ph in range(4):
                piece = outs[ph][:, 128 * t:128 * t + 128]
                if ph != j:
                    piece = pltpu.roll(piece, (32 * (ph - j)) % 128, 1)
                tile = piece if tile is None else jnp.where(block == ph, piece, tile)
            fin[f, 4 * t + j] = tile
            parts = [tile[8 * m:8 * m + 8] for m in range(3)]
            parts = [pltpu.roll(v, 8 * m + 64 * f, 1) if m or f else v for m, v in enumerate(parts)]
            rot[f, 4 * t + j] = jnp.concatenate(parts, 0)
    fin[f, TILES - 1] = jnp.zeros((CO, 128), F32)
    rot[f, TILES - 1] = jnp.zeros((CO, 128), F32)


def cut_strips(f, starts, fin, rot, send):
    lane = col_iota((1, 128))
    row = (lane % 32) // PW * 2 + lane // 64
    for to in range(N):
        start = starts[to]
        tile, off = start // 8, start % 8
        main = jnp.where(row >= off, fin[f, tile], fin[f, tile + 1])
        if f == 0:
            send[to] = main.astype(BF16)
            continue
        slot = (lane // 8 + 16 - (off % 2 * 8 + off // 2)) % 16
        tail = None
        for g in range(FR):
            ninth = rot[g, tile + 1]
            for m in range(3):
                part = ninth[8 * m:8 * m + 8]
                tail = part if tail is None else jnp.where((slot // 8 == g) & (slot % 4 == m), part, tail)
        send[to] = jnp.concatenate([main, tail], 0).astype(BF16)


def strip_pick(start, count):
    shape = (9 * 16, 256)
    p, lane = row_iota(shape), col_iota(shape)
    k, col = p // 16, p % 16
    row = (start + k) % 8
    at = row % 2 * 64 + col % 2 * 32 + row // 2 * PW + col // 2 + jnp.where(k == 8, 128, 0)
    return jnp.where((lane == at) & (k < count), 1.0, 0.0).astype(BF16)


def main_kernel(
    rows_ref, tok_ref, f_ref, b1_ref, gain_ref, w_ref, b2_ref, recv0, recv1, pick,
    rows, tokv, fv, b1v, gainv, b2v, pack, tok_all, ft, ft0, ghalf, b2col, place, wcat, xp, hid, prod, fin, rot, send0, send1,
    starts, local_sem, ok, hub_send, tok_send, tok_recv, out_sent, out_recv,
):
    me = lax.axis_index("sp")
    early = me < NF
    barrier = pltpu.get_barrier_semaphore()

    def greet(i):
        pl.semaphore_signal(barrier, inc=1, device_id=peer(i), device_id_type=MESH)

    def tok_copy(to):
        return pltpu.make_async_remote_copy(
            src_ref=pack, dst_ref=tok_all.at[me], send_sem=tok_send, recv_sem=tok_recv.at[me // NF],
            device_id=peer(to), device_id_type=MESH,
        )

    first_core = me % 2 == 0

    @pl.when(early)
    def _():
        for chip in range(NF // 2):
            @pl.when(me != 2 * chip)
            def _():
                greet(2 * chip)

        for_others(me, NF, N, greet)

    @pl.when(jnp.logical_not(early))
    def _():
        greet(jnp.where(me < 10, 5, jnp.where(me < 12, 7, 1)))
        for_others(me, NF, N, greet)

    copies = [
        (tok_ref, tokv), (f_ref.at[1], fv.at[0]), (f_ref.at[2], fv.at[1]), (b1_ref, b1v.at[0]), (gain_ref, gainv.at[0]), (b2_ref, b2v.at[0]),
        (w_ref.at[1], wcat.at[:, 0:C2]), (w_ref.at[2], wcat.at[:, C2:2 * C2]), (rows_ref, rows),
    ]
    copies = [pltpu.make_async_copy(s, d, local_sem.at[i]) for i, (s, d) in enumerate(copies)]
    for copy in copies:
        copy.start()

    copies[0].wait()
    tokens = tokv[...].astype(F32)
    right = jnp.concatenate([tokens[HALF:], jnp.zeros((2 * HALF - TOK, 64), F32)], 0)
    block = jnp.concatenate([tokens[:HALF], right], 1).astype(BF16)
    pack[...] = block
    tok_all[me] = block

    @pl.when(early & first_core)
    def _():
        pl.semaphore_wait(barrier, NF - 1)
        pl.semaphore_signal(ok, inc=1, device_id=peer(me + 1), device_id_type=MESH)

    @pl.when(early & jnp.logical_not(first_core))
    def _():
        pl.semaphore_wait(ok, 1)

    @pl.when(early)
    def _():
        for_others(me, 0, NF, lambda i: tok_copy(i).start())

    @pl.when(jnp.logical_not(early))
    def _():
        pl.semaphore_wait(barrier, N - 1)
        for_others(me, NF, N, lambda i: tok_copy(i).start())
        for_others(me, 0, NF, lambda i: tok_copy(i).start())

    for copy in copies[1:]:
        copy.wait()

    def begin(i, start):
        starts[i] = start
        return start + rows[i]

    lax.fori_loop(0, N, begin, 0)
    prepare(fv, b1v, gainv, b2v, me, ft, ft0, ghalf, b2col, place, xp)
    pick[...] = strip_pick(starts[me], rows[me])

    after = lax.rem(me + 1, N)

    def tok_wait(f, count):
        slabs = tok_all.at[pl.ds(0, count)]
        pltpu.make_async_remote_copy(
            src_ref=slabs, dst_ref=slabs, send_sem=tok_send, recv_sem=tok_recv.at[f], device_id=peer(after), device_id_type=MESH
        ).wait_recv()

    def out_copy(f, source, target, to):
        return pltpu.make_async_remote_copy(
            src_ref=source, dst_ref=target, send_sem=out_sent.at[f], recv_sem=out_recv.at[f],
            device_id=peer(to), device_id_type=MESH,
        )

    def out_send(f, low, high):
        send, recv = ((send0, recv0), (send1, recv1))[f]
        for_others(me, low, high, lambda to: out_copy(f, send.at[to], recv.at[me], to).start())

    def hub_copy(to):
        slabs = tok_all.at[pl.ds(0, NF)]
        return pltpu.make_async_remote_copy(
            src_ref=slabs, dst_ref=slabs, send_sem=hub_send, recv_sem=tok_recv.at[0], device_id=peer(to), device_id_type=MESH
        )

    @pl.when(early)
    def _():
        tok_wait(0, NF - 1)

    @pl.when(me == 1)
    def _():
        pl.semaphore_wait(barrier, 4)
        for to in range(12, 16):
            hub_copy(to).start()

    @pl.when((me == 5) | (me == 7))
    def _():
        pl.semaphore_wait(barrier, 2)
        hub_copy(me + 3).start()
        hub_copy(me + 4).start()

    for f, (send, recv) in enumerate(((send0, recv0), (send1, recv1))):
        if f == 0:
            @pl.when(jnp.logical_not(early))
            def _():
                tok_wait(0, NF)
        else:
            @pl.when(early)
            def _():
                tok_wait(1, NF)
                out_send(0, NF, N)

            @pl.when(jnp.logical_not(early))
            def _():
                tok_wait(1, NF - 1)

        patches(f, tok_all, place, xp)
        convolve(f, xp, ft, ft0, ghalf, wcat, hid, prod)
        gather_taps(f, me, prod, b2col, fin, rot)
        cut_strips(f, starts, fin, rot, send)

        if f == 0:
            out_send(0, 0, NF)

            @pl.when(jnp.logical_not(early))
            def _():
                out_send(0, NF, N)
        else:
            out_send(1, 0, N)
        recv[me] = send[me]

    def tok_sent(count, sem):
        slabs = tok_all.at[pl.ds(0, count)]
        pltpu.make_async_remote_copy(
            src_ref=slabs, dst_ref=slabs, send_sem=sem, recv_sem=tok_recv.at[0], device_id=peer(after), device_id_type=MESH
        ).wait_send()

    @pl.when(early)
    def _():
        tok_sent(NF - 1, tok_send)

    @pl.when(jnp.logical_not(early))
    def _():
        tok_sent(N - 1, tok_send)

    @pl.when(me == 1)
    def _():
        tok_sent(N, hub_send)
        tok_sent(N, hub_send)

    @pl.when((me == 5) | (me == 7))
    def _():
        tok_sent(N, hub_send)

    for f, (send, recv) in enumerate(((send0, recv0), (send1, recv1))):
        out_copy(f, send.at[pl.ds(0, N - 1)], recv.at[pl.ds(0, N - 1)], after).wait()


def exchange(strip_rows, tokens, f, b1, gain, w, b2):
    hbm = pl.BlockSpec(memory_space=pltpu.HBM)
    return pl.pallas_call(
        main_kernel,
        out_shape=(pltpu.VMEM((N, CO, 128), BF16), pltpu.VMEM((N, CO + 8, 128), BF16), pltpu.VMEM((9 * 16, 256), BF16)),
        in_specs=[hbm] * 7,
        out_specs=(pl.BlockSpec(memory_space=pltpu.VMEM),) * 3,
        scratch_shapes=[
            pltpu.SMEM((N,), jnp.int32),
            pltpu.VMEM((TOK, 64), BF16),
            pltpu.VMEM((2, 144, C2), BF16),
            pltpu.VMEM((1, C2), F32),
            pltpu.VMEM((1, C2), F32),
            pltpu.VMEM((1, C2), F32),
            pltpu.VMEM((HALF, 128), BF16),
            pltpu.VMEM((N, HALF, 128), BF16),
            pltpu.VMEM((C2, 304), BF16),
            pltpu.VMEM((C2, 160), BF16),
            pltpu.VMEM((C2, 128), F32),
            pltpu.VMEM((C2, 128), F32),
            pltpu.VMEM((2, 8 * HALF, FL), BF16),
            pltpu.VMEM((9 * CO, 2 * C2), BF16),
            pltpu.VMEM((304, 4 * FL), BF16),
            pltpu.VMEM((2 * C2, 4 * FL), BF16),
            pltpu.VMEM((9 * CO, 4 * FL), F32),
            pltpu.VMEM((FR, TILES, CO, 128), F32),
            pltpu.VMEM((FR, TILES, CO, 128), F32),
            pltpu.VMEM((N, CO, 128), BF16),
            pltpu.VMEM((N, CO + 8, 128), BF16),
            pltpu.SMEM((N,), jnp.int32),
            pltpu.SemaphoreType.DMA((9,)),
            pltpu.SemaphoreType.REGULAR,
            pltpu.SemaphoreType.DMA,
            pltpu.SemaphoreType.DMA,
            pltpu.SemaphoreType.DMA((FR,)),
            pltpu.SemaphoreType.DMA((FR,)),
            pltpu.SemaphoreType.DMA((FR,)),
        ],
        compiler_params=pltpu.CompilerParams(collective_id=0, has_side_effects=True, vmem_limit_bytes=40 << 20),
    )(*(pltpu.with_memory_space_constraint(v, pltpu.HBM) for v in (strip_rows, tokens, f, b1, gain, w, b2)))


def assemble_kernel(pick, recv0, recv1, out):
    tail = recv1[...].astype(F32)[:, CO:]
    for f, recv in enumerate((recv0, recv1)):
        main = recv[...].astype(F32)[:, :CO].reshape(C2, 128)
        turns = [8 * m + 64 * f for m in range(3)]
        ninth = jnp.concatenate([pltpu.roll(tail, 128 - n, 2) if n else tail for n in turns], 1).reshape(C2, 128)
        both = jnp.concatenate([main, ninth], 1).astype(BF16)
        strip = lax.dot_general(pick[...], both, (((1,), (1,)), ((), ())), preferred_element_type=F32)
        out[0, f] = strip.astype(BF16).reshape(9, 16, C2)


def assemble(pick, recv0, recv1):
    vmem = pl.BlockSpec(memory_space=pltpu.VMEM)
    return pl.pallas_call(
        assemble_kernel,
        out_shape=jax.ShapeDtypeStruct((1, FR, 9, 16, C2), BF16),
        in_specs=[vmem] * 3,
        out_specs=vmem,
        compiler_params=pltpu.CompilerParams(vmem_limit_bytes=20 << 20),
    )(pick, recv0, recv1)


def per_device(tokens, strip_rows, first_filter, first_bias, norm_gain, second_filter, second_bias):
    f = first_filter.reshape(3, 9 * C, C2)
    w = jnp.transpose(second_filter, (0, 1, 2, 4, 3)).reshape(3, 9 * CO, C2)
    recv0, recv1, pick = exchange(strip_rows, tokens, f, first_bias, norm_gain, w, second_bias)
    return assemble(pick, recv0, recv1)


def solution(mesh):
    in_specs = (P(("req", "sp"), None), P(), P(), P(), P(), P(None, None, None, None, "sp"), P())
    out_specs = P(("req", "sp"), None, None, None, None)
    return jax.shard_map(
        per_device, mesh=mesh, in_specs=in_specs, out_specs=out_specs, check_vma=False
    )
```

```python
import jax
import jax.numpy as jnp
from jax import lax
from jax.experimental import pallas as pl
from jax.experimental.pallas import tpu as pltpu
from jax.sharding import PartitionSpec as P

C = 16
FR = 2
PH = 45
PW = 8
N = 16
NF = N // FR
FIRST = 8
TOK = FR * PH * PW // N
HALF = 24
FL = 384
LIVE = PH * PW
C2 = 384
CO = 24
TILES = 13
CHUNK = 256
MESH = pl.DeviceIdType.MESH
F32, BF16 = jnp.float32, jnp.bfloat16


def peer(i):
    return {"sp": i}


def for_others(me, low, high, act):
    def step(i, carry):
        @pl.when(i != me)
        def _():
            act(i)

        return carry

    lax.fori_loop(low, high, step, 0)


def col_iota(shape):
    return lax.broadcasted_iota(jnp.int32, shape, len(shape) - 1)


def row_iota(shape):
    return lax.broadcasted_iota(jnp.int32, shape, len(shape) - 2)


def shift_of(phase, d):
    moved = phase + d
    return moved % 2, moved // 2


def prepare(f_ref, b1_ref, gain_ref, b2_ref, me, ft, ft0, ghalf, b2col, place, xp):
    tap1, tap2 = f_ref[0].astype(F32), f_ref[1].astype(F32)
    bias = b1_ref[...]
    hi = bias.astype(BF16).astype(F32)
    mid = (bias - hi).astype(BF16).astype(F32)
    low = bias - hi - mid
    rows = row_iota((16, C2))
    bias_rows = jnp.where(rows == 0, hi, jnp.where(rows == 1, mid, jnp.where(rows == 2, low, 0.0)))
    ft[...] = jnp.concatenate([tap2, bias_rows, tap1, jnp.zeros((80, C2), F32)], 0).T[:, :304].astype(BF16)
    ft0[...] = jnp.concatenate([bias_rows, tap2, jnp.zeros((96, C2), F32)], 0).T[:, :160].astype(BF16)
    ghalf[...] = jnp.broadcast_to(gain_ref[...] * 0.5, (128, C2)).T
    b2col[...] = jnp.broadcast_to(b2_ref[...], (128, C2)).T
    shape = (8 * HALF, FL)
    token = row_iota(shape)
    src, i = token // HALF, token % HALF
    lane = col_iota(shape)
    one, zero = jnp.ones(shape, F32), jnp.zeros(shape, F32)
    place[0] = jnp.where(lane == src * TOK + i, one, zero).astype(BF16)
    place[1] = jnp.where((lane == src * TOK + HALF + i) & (i < TOK - HALF), one, zero).astype(BF16)
    xp[144:160, :] = jnp.ones((16, 4 * FL), BF16)


def patches(f, tok_all, place, xp):
    blocks = tok_all[8 * f:8 * f + 8].astype(F32).reshape(8 * HALF, 128).T.astype(BF16)
    grid = jnp.dot(blocks[:64], place[0], preferred_element_type=F32) + jnp.dot(blocks[64:], place[1], preferred_element_type=F32)
    q = col_iota((1, FL)) % PW
    for a2 in range(2):
        for b2 in range(2):
            at = (a2 * 2 + b2) * C
            field = grid[at:at + C]
            moved = {}
            for sr in ((0, -1) if a2 == 1 else (0, 1)):
                for sq in ((0, -1) if b2 == 1 else (0, 1)):
                    piece = field
                    if sr or sq:
                        piece = pltpu.roll(piece, (-(PW * sr + sq)) % FL, 1)
                    if sq:
                        piece = jnp.where(q == (0 if sq < 0 else PW - 1), 0.0, piece)
                    moved[sr, sq] = piece.astype(BF16)
            for a in range(2):
                for b in range(2):
                    for dy in range(3):
                        for dx in range(3):
                            sa, sr = shift_of(a, dy - 1)
                            sb, sq = shift_of(b, dx - 1)
                            if (sa, sb) == (a2, b2):
                                row = (160 if f == 0 else 0) + (dy * 3 + dx) * C
                                ph = a * 2 + b
                                xp[row:row + C, ph * FL:(ph + 1) * FL] = moved[sr, sq]


def convolve(f, xp, ft, ft0, ghalf, wcat, hid, prod, between=None):
    def first_of(at):
        lanes = slice(at, at + CHUNK)
        if f == 0:
            return jnp.dot(ft0[...], xp[144:304, lanes], preferred_element_type=F32)
        return jnp.dot(ft[...], xp[:, lanes], preferred_element_type=F32)

    def second_of(at):
        lanes = slice(at, at + CHUNK)
        if f == 0:
            prod[f, :, lanes] = jnp.dot(wcat[:, C2:], hid[0:C2, lanes], preferred_element_type=F32)
        else:
            prod[f, :, lanes] = jnp.dot(wcat[...], hid[:, lanes], preferred_element_type=F32)

    def act(at, first):
        lanes = slice(at, at + CHUNK)
        mean = jnp.sum(first * first, axis=0, keepdims=True) * (1.0 / C2)
        live = (col_iota((1, CHUNK)) + at) % FL < LIVE
        scale = jnp.where(live, lax.rsqrt(mean + 1e-6), 0.0)
        gain = jnp.concatenate([ghalf[...]] * (CHUNK // 128), 1)
        u = first * scale * gain
        hid[f * C2:(f + 1) * C2, lanes] = (u + u * jnp.tanh(u)).astype(BF16)

    ats = list(range(0, 4 * FL, CHUNK))
    ready = first_of(ats[0])
    for n, at in enumerate(ats):
        ahead = first_of(ats[n + 1]) if n + 1 < len(ats) else None
        act(at, ready)
        if n:
            second_of(ats[n - 1])
        if between is not None and n == 1:
            between()
        ready = ahead
    second_of(ats[-1])


def gather_taps(f, me, prod, b2col, fin, rot):
    q = col_iota((1, FL)) % PW
    bias = b2col[pl.ds(pl.multiple_of(me * CO, 8), CO), :]
    bias = jnp.concatenate([bias] * (FL // 128), 1)
    outs = []
    for a in range(2):
        for b in range(2):
            sums = {}
            for dy in range(3):
                for dx in range(3):
                    sa, sr = shift_of(a, dy - 1)
                    sb, sq = shift_of(b, dx - 1)
                    tap, ph = dy * 3 + dx, sa * 2 + sb
                    term = prod[f, tap * CO:(tap + 1) * CO, ph * FL:(ph + 1) * FL]
                    sums[sr, sq] = sums[sr, sq] + term if (sr, sq) in sums else term
            sr, sq = (-1, 1)[a], (-1, 1)[b]
            side = sums[0, sq] + pltpu.roll(sums[sr, sq], (-PW * sr) % FL, 1)
            side = pltpu.roll(side, (-sq) % FL, 1)
            side = jnp.where(q == (0 if sq < 0 else PW - 1), 0.0, side)
            outs.append(sums[0, 0] + pltpu.roll(sums[sr, 0], (-PW * sr) % FL, 1) + side + bias)
    block = col_iota((1, 128)) // 32
    for t in range(FL // 128):
        for j in range(4):
            tile = None
            for ph in range(4):
                piece = outs[ph][:, 128 * t:128 * t + 128]
                if ph != j:
                    piece = pltpu.roll(piece, (32 * (ph - j)) % 128, 1)
                tile = piece if tile is None else jnp.where(block == ph, piece, tile)
            fin[f, 4 * t + j] = tile
            parts = [tile[8 * m:8 * m + 8] for m in range(3)]
            parts = [pltpu.roll(v, 8 * m + 64 * f, 1) if m or f else v for m, v in enumerate(parts)]
            rot[f, 4 * t + j] = jnp.concatenate(parts, 0)
    fin[f, TILES - 1] = jnp.zeros((CO, 128), F32)
    rot[f, TILES - 1] = jnp.zeros((CO, 128), F32)


def mask_strips(rows, starts, tiles, keep, slots):
    lane = col_iota((8, 128))
    row = ((lane & 31) >> 3) * 2 + (lane >> 6)

    def step(to, start):
        off = start & 7
        starts[to] = start
        tiles[to] = start >> 3
        keep[to] = (row >= off).astype(jnp.int32)
        slot = ((lane >> 3) + 16 - ((off & 1) * 8 + (off >> 1))) & 15
        slots[to] = (slot >> 3) * 3 + (slot & 3)
        return start + rows[to]

    lax.fori_loop(0, N, step, 0)


def cut_strips(f, tiles, keep, slots, fin, rot, send):
    for to in range(N):
        tile = tiles[to]
        first = keep[to] > 0
        one, two = fin[f, tile], fin[f, tile + 1]
        parts = [jnp.where(first, one[8 * m:8 * m + 8], two[8 * m:8 * m + 8]) for m in range(3)]
        if f == 1:
            slot = slots[to]
            tail = rot[0, tile + 1][:8]
            for n in range(1, 6):
                m = n % 3
                tail = jnp.where(slot == n, rot[n // 3, tile + 1][8 * m:8 * m + 8], tail)
            parts.append(tail)
        send[to] = jnp.concatenate(parts, 0).astype(BF16)


def strip_pick(start, count):
    shape = (9 * 16, 256)
    p, lane = row_iota(shape), col_iota(shape)
    k, col = p // 16, p % 16
    row = (start + k) % 8
    at = row % 2 * 64 + col % 2 * 32 + row // 2 * PW + col // 2 + jnp.where(k == 8, 128, 0)
    return jnp.where((lane == at) & (k < count), 1.0, 0.0).astype(BF16)


def main_kernel(
    rows_ref, tok_ref, f_ref, b1_ref, gain_ref, w_ref, b2_ref, recv0, recv1, pick,
    rows, tokv, fv, b1v, gainv, b2v, pack, tok_all, ft, ft0, ghalf, b2col, place, wcat, xp, hid, prod, fin, rot, send0, send1,
    starts, tiles, keep, slots, local_sem, ok, hub_send, tok_send, tok_recv, out_sent, out_recv,
):
    me = lax.axis_index("sp")
    early = me < NF
    barrier = pltpu.get_barrier_semaphore()

    def greet(i):
        pl.semaphore_signal(barrier, inc=1, device_id=peer(i), device_id_type=MESH)

    def tok_copy(to):
        return pltpu.make_async_remote_copy(
            src_ref=pack, dst_ref=tok_all.at[me], send_sem=tok_send, recv_sem=tok_recv.at[jnp.minimum(me // 2, 4)],
            device_id=peer(to), device_id_type=MESH,
        )

    first_core = me % 2 == 0

    @pl.when(early)
    def _():
        for chip in range(NF // 2):
            @pl.when(me != 2 * chip)
            def _():
                greet(2 * chip)

        for_others(me, NF, N, greet)

    @pl.when(jnp.logical_not(early))
    def _():
        greet(jnp.where(me < 10, 5, jnp.where(me < 12, 7, 1)))
        for_others(me, NF, N, greet)

    copies = [
        (tok_ref, tokv), (f_ref.at[1], fv.at[0]), (f_ref.at[2], fv.at[1]), (b1_ref, b1v.at[0]), (gain_ref, gainv.at[0]), (b2_ref, b2v.at[0]),
        (w_ref.at[1], wcat.at[:, 0:C2]), (w_ref.at[2], wcat.at[:, C2:2 * C2]), (rows_ref, rows),
    ]
    copies = [pltpu.make_async_copy(s, d, local_sem.at[i]) for i, (s, d) in enumerate(copies)]
    for copy in copies:
        copy.start()

    copies[0].wait()
    tokens = tokv[...].astype(F32)
    right = jnp.concatenate([tokens[HALF:], jnp.zeros((2 * HALF - TOK, 64), F32)], 0)
    block = jnp.concatenate([tokens[:HALF], right], 1).astype(BF16)
    pack[...] = block
    tok_all[me] = block

    @pl.when(early & first_core)
    def _():
        pl.semaphore_wait(barrier, NF - 1)
        pl.semaphore_signal(ok, inc=1, device_id=peer(me + 1), device_id_type=MESH)

    @pl.when(early & jnp.logical_not(first_core))
    def _():
        pl.semaphore_wait(ok, 1)

    @pl.when(early)
    def _():
        for_others(me, 0, NF, lambda i: tok_copy(i).start())

    @pl.when(jnp.logical_not(early))
    def _():
        pl.semaphore_wait(barrier, N - 1)
        for_others(me, NF, N, lambda i: tok_copy(i).start())
        for_others(me, 0, NF, lambda i: tok_copy(i).start())

    for copy in copies[1:]:
        copy.wait()

    mask_strips(rows, starts, tiles, keep, slots)
    prepare(fv, b1v, gainv, b2v, me, ft, ft0, ghalf, b2col, place, xp)
    pick[...] = strip_pick(starts[me], rows[me])

    after = lax.rem(me + 1, N)

    def tok_wait(f, count):
        slabs = tok_all.at[pl.ds(0, count)]
        pltpu.make_async_remote_copy(
            src_ref=slabs, dst_ref=slabs, send_sem=tok_send, recv_sem=tok_recv.at[f], device_id=peer(after), device_id_type=MESH
        ).wait_recv()

    def out_copy(f, source, target, to):
        return pltpu.make_async_remote_copy(
            src_ref=source, dst_ref=target, send_sem=out_sent.at[f], recv_sem=out_recv.at[f],
            device_id=peer(to), device_id_type=MESH,
        )

    def out_start(f, i):
        send, recv = ((send0, recv0), (send1, recv1))[f]
        twin = me + 1 - 2 * (me % 2)
        at = i + (i >= twin).astype(jnp.int32)
        to = at + 1 - 2 * (at % 2)
        out_copy(f, send.at[to], recv.at[me], to).start()

    def finish(f):
        send, recv = ((send0, recv0), (send1, recv1))[f]
        gather_taps(f, me, prod, b2col, fin, rot)
        cut_strips(f, tiles, keep, slots, fin, rot, send)
        for i in range(N - 1):
            if f == 1 and i >= FIRST:
                out_start(0, i)
            if f == 1 or i < FIRST:
                out_start(f, i)
        recv[me] = send[me]

    def hub_pass(clients, low, high):
        slabs = tok_all.at[pl.ds(low, high - low)]
        for to in clients:
            pltpu.make_async_remote_copy(
                src_ref=slabs, dst_ref=slabs, send_sem=hub_send, recv_sem=tok_recv.at[0], device_id=peer(to), device_id_type=MESH
            ).start()

    @pl.when(me == 1)
    def _():
        clients = range(12, 16)
        tok_wait(0, 1)
        tok_wait(1, 2)
        pl.semaphore_wait(barrier, 4)
        hub_pass(clients, 0, 4)
        tok_wait(2, 2)
        hub_pass(clients, 4, 6)
        tok_wait(3, 2)
        hub_pass(clients, 6, 8)

    @pl.when(me == 5)
    def _():
        clients = (8, 9)
        tok_wait(2, 1)
        tok_wait(1, 2)
        pl.semaphore_wait(barrier, 2)
        hub_pass(clients, 2, 6)
        tok_wait(3, 2)
        hub_pass(clients, 6, 8)
        tok_wait(0, 2)
        hub_pass(clients, 0, 2)

    @pl.when(me == 7)
    def _():
        clients = (10, 11)
        tok_wait(3, 1)
        tok_wait(2, 2)
        pl.semaphore_wait(barrier, 2)
        hub_pass(clients, 4, 8)
        tok_wait(1, 2)
        hub_pass(clients, 2, 4)
        tok_wait(0, 2)
        hub_pass(clients, 0, 2)

    @pl.when(early & (first_core | (me == 3)))
    def _():
        for chip in range(4):
            @pl.when(me // 2 == chip)
            def _():
                tok_wait(chip, 1)

            @pl.when(me // 2 != chip)
            def _():
                tok_wait(chip, 2)

    @pl.when(jnp.logical_not(early))
    def _():
        tok_wait(0, NF)

    patches(0, tok_all, place, xp)
    convolve(0, xp, ft, ft0, ghalf, wcat, hid, prod)

    @pl.when(early)
    def _():
        tok_wait(4, NF)

    @pl.when(jnp.logical_not(early))
    def _():
        tok_wait(4, NF - 1)

    patches(1, tok_all, place, xp)
    convolve(1, xp, ft, ft0, ghalf, wcat, hid, prod, lambda: finish(0))
    finish(1)

    def tok_sent(count, sem):
        slabs = tok_all.at[pl.ds(0, count)]
        pltpu.make_async_remote_copy(
            src_ref=slabs, dst_ref=slabs, send_sem=sem, recv_sem=tok_recv.at[0], device_id=peer(after), device_id_type=MESH
        ).wait_send()

    @pl.when(early)
    def _():
        tok_sent(NF - 1, tok_send)

    @pl.when(jnp.logical_not(early))
    def _():
        tok_sent(N - 1, tok_send)

    @pl.when(me == 1)
    def _():
        tok_sent(N, hub_send)
        tok_sent(N, hub_send)

    @pl.when((me == 5) | (me == 7))
    def _():
        tok_sent(N, hub_send)

    for f, (send, recv) in enumerate(((send0, recv0), (send1, recv1))):
        out_copy(f, send.at[pl.ds(0, N - 1)], recv.at[pl.ds(0, N - 1)], after).wait()


def exchange(strip_rows, tokens, f, b1, gain, w, b2):
    hbm = pl.BlockSpec(memory_space=pltpu.HBM)
    return pl.pallas_call(
        main_kernel,
        out_shape=(pltpu.VMEM((N, CO, 128), BF16), pltpu.VMEM((N, CO + 8, 128), BF16), pltpu.VMEM((9 * 16, 256), BF16)),
        in_specs=[hbm] * 7,
        out_specs=(pl.BlockSpec(memory_space=pltpu.VMEM),) * 3,
        scratch_shapes=[
            pltpu.SMEM((N,), jnp.int32),
            pltpu.VMEM((TOK, 64), BF16),
            pltpu.VMEM((2, 144, C2), BF16),
            pltpu.VMEM((1, C2), F32),
            pltpu.VMEM((1, C2), F32),
            pltpu.VMEM((1, C2), F32),
            pltpu.VMEM((HALF, 128), BF16),
            pltpu.VMEM((N, HALF, 128), BF16),
            pltpu.VMEM((C2, 304), BF16),
            pltpu.VMEM((C2, 160), BF16),
            pltpu.VMEM((C2, 128), F32),
            pltpu.VMEM((C2, 128), F32),
            pltpu.VMEM((2, 8 * HALF, FL), BF16),
            pltpu.VMEM((9 * CO, 2 * C2), BF16),
            pltpu.VMEM((304, 4 * FL), BF16),
            pltpu.VMEM((2 * C2, 4 * FL), BF16),
            pltpu.VMEM((FR, 9 * CO, 4 * FL), F32),
            pltpu.VMEM((FR, TILES, CO, 128), F32),
            pltpu.VMEM((FR, TILES, CO, 128), F32),
            pltpu.VMEM((N, CO, 128), BF16),
            pltpu.VMEM((N, CO + 8, 128), BF16),
            pltpu.SMEM((N,), jnp.int32),
            pltpu.SMEM((N,), jnp.int32),
            pltpu.VMEM((N, 8, 128), jnp.int32),
            pltpu.VMEM((N, 8, 128), jnp.int32),
            pltpu.SemaphoreType.DMA((9,)),
            pltpu.SemaphoreType.REGULAR,
            pltpu.SemaphoreType.DMA,
            pltpu.SemaphoreType.DMA,
            pltpu.SemaphoreType.DMA((5,)),
            pltpu.SemaphoreType.DMA((FR,)),
            pltpu.SemaphoreType.DMA((FR,)),
        ],
        compiler_params=pltpu.CompilerParams(collective_id=0, has_side_effects=True, vmem_limit_bytes=40 << 20),
    )(*(pltpu.with_memory_space_constraint(v, pltpu.HBM) for v in (strip_rows, tokens, f, b1, gain, w, b2)))


def assemble_kernel(pick, recv0, recv1, out, strips, sent):
    tail = recv1[...].astype(F32)[:, CO:]
    copies = []
    for f, recv in enumerate((recv0, recv1)):
        main = recv[...].astype(F32)[:, :CO].reshape(C2, 128)
        turns = [8 * m + 64 * f for m in range(3)]
        ninth = jnp.concatenate([pltpu.roll(tail, 128 - n, 2) if n else tail for n in turns], 1).reshape(C2, 128)
        both = jnp.concatenate([main, ninth], 1).astype(BF16)
        strip = lax.dot_general(pick[...], both, (((1,), (1,)), ((), ())), preferred_element_type=F32)
        strips[f] = strip.astype(BF16).reshape(9, 16, C2)
        copies.append(pltpu.make_async_copy(strips.at[f], out.at[0, f], sent.at[f]))
        copies[f].start()
    for copy in copies:
        copy.wait()


def assemble(pick, recv0, recv1):
    vmem = pl.BlockSpec(memory_space=pltpu.VMEM)
    return pl.pallas_call(
        assemble_kernel,
        out_shape=jax.ShapeDtypeStruct((1, FR, 9, 16, C2), BF16),
        in_specs=[vmem] * 3,
        out_specs=pl.BlockSpec(memory_space=pl.ANY),
        scratch_shapes=[pltpu.VMEM((FR, 9, 16, C2), BF16), pltpu.SemaphoreType.DMA((FR,))],
        compiler_params=pltpu.CompilerParams(vmem_limit_bytes=20 << 20),
    )(pick, recv0, recv1)


def per_device(tokens, strip_rows, first_filter, first_bias, norm_gain, second_filter, second_bias):
    f = first_filter.reshape(3, 9 * C, C2)
    w = jnp.transpose(second_filter, (0, 1, 2, 4, 3)).reshape(3, 9 * CO, C2)
    recv0, recv1, pick = exchange(strip_rows, tokens, f, first_bias, norm_gain, w, second_bias)
    return assemble(pick, recv0, recv1)


def solution(mesh):
    in_specs = (P(("req", "sp"), None), P(), P(), P(), P(), P(None, None, None, None, "sp"), P())
    out_specs = P(("req", "sp"), None, None, None, None)
    return jax.shard_map(
        per_device, mesh=mesh, in_specs=in_specs, out_specs=out_specs, check_vma=False
    )
```

```python
import jax
import jax.numpy as jnp
from jax import lax
from jax.experimental import pallas as pl
from jax.experimental.pallas import tpu as pltpu
from jax.sharding import PartitionSpec as P

C = 16
FR = 2
PH = 45
PW = 8
N = 16
NF = N // FR
FIRST = 4
TOK = FR * PH * PW // N
HALF = 24
FL = 384
LIVE = PH * PW
C2 = 384
CO = 24
TILES = 13
CHUNK = 256
MESH = pl.DeviceIdType.MESH
F32, BF16 = jnp.float32, jnp.bfloat16


def peer(i):
    return {"sp": i}


def for_others(me, low, high, act):
    def step(i, carry):
        @pl.when(i != me)
        def _():
            act(i)

        return carry

    lax.fori_loop(low, high, step, 0)


def col_iota(shape):
    return lax.broadcasted_iota(jnp.int32, shape, len(shape) - 1)


def row_iota(shape):
    return lax.broadcasted_iota(jnp.int32, shape, len(shape) - 2)


def shift_of(phase, d):
    moved = phase + d
    return moved % 2, moved // 2


def prepare(f_ref, b1_ref, gain_ref, b2_ref, me, now, back, ghalf, b2col, place, xp):
    tap1, tap2 = f_ref[0].astype(F32), f_ref[1].astype(F32)
    bias = b1_ref[...]
    hi = bias.astype(BF16).astype(F32)
    mid = (bias - hi).astype(BF16).astype(F32)
    low = bias - hi - mid
    rows = row_iota((16, C2))
    bias_rows = jnp.where(rows == 0, hi, jnp.where(rows == 1, mid, jnp.where(rows == 2, low, 0.0)))
    now[...] = jnp.concatenate([tap2, bias_rows, jnp.zeros((96, C2), F32)], 0).T[:, :160].astype(BF16)
    back[...] = jnp.concatenate([tap1, jnp.zeros((112, C2), F32)], 0).T[:, :144].astype(BF16)
    ghalf[...] = jnp.broadcast_to(gain_ref[...] * 0.5, (128, C2)).T
    b2col[...] = jnp.broadcast_to(b2_ref[...], (128, C2)).T
    shape = (8 * HALF, FL)
    token = row_iota(shape)
    src, i = token // HALF, token % HALF
    lane = col_iota(shape)
    one, zero = jnp.ones(shape, F32), jnp.zeros(shape, F32)
    place[0] = jnp.where(lane == src * TOK + i, one, zero).astype(BF16)
    place[1] = jnp.where((lane == src * TOK + HALF + i) & (i < TOK - HALF), one, zero).astype(BF16)
    xp[144:160, :] = jnp.ones((16, 4 * FL), BF16)
    xp[304:320, :] = jnp.ones((16, 4 * FL), BF16)


def patches(f, tok_all, place, xp):
    blocks = tok_all[8 * f:8 * f + 8].astype(F32).reshape(8 * HALF, 128).T.astype(BF16)
    grid = jnp.dot(blocks[:64], place[0], preferred_element_type=F32) + jnp.dot(blocks[64:], place[1], preferred_element_type=F32)
    q = col_iota((1, FL)) % PW
    for a2 in range(2):
        for b2 in range(2):
            at = (a2 * 2 + b2) * C
            field = grid[at:at + C]
            moved = {}
            for sr in ((0, -1) if a2 == 1 else (0, 1)):
                for sq in ((0, -1) if b2 == 1 else (0, 1)):
                    piece = field
                    if sr or sq:
                        piece = pltpu.roll(piece, (-(PW * sr + sq)) % FL, 1)
                    if sq:
                        piece = jnp.where(q == (0 if sq < 0 else PW - 1), 0.0, piece)
                    moved[sr, sq] = piece.astype(BF16)
            for a in range(2):
                for b in range(2):
                    for dy in range(3):
                        for dx in range(3):
                            sa, sr = shift_of(a, dy - 1)
                            sb, sq = shift_of(b, dx - 1)
                            if (sa, sb) == (a2, b2):
                                row = (160 if f == 0 else 0) + (dy * 3 + dx) * C
                                ph = a * 2 + b
                                xp[row:row + C, ph * FL:(ph + 1) * FL] = moved[sr, sq]


def convolve_own(xp, now, own):
    for at in range(0, 4 * FL, CHUNK):
        own[:, at:at + CHUNK] = jnp.dot(now[...], xp[0:160, at:at + CHUNK], preferred_element_type=F32)


def convolve(f, xp, now, back, own, ghalf, wcat, hid, prod, between=None):
    def first_of(at):
        lanes = slice(at, at + CHUNK)
        if f == 0:
            return jnp.dot(now[...], xp[160:320, lanes], preferred_element_type=F32)
        return jnp.dot(back[...], xp[160:304, lanes], preferred_element_type=F32) + own[:, lanes]

    def second_of(at):
        lanes = slice(at, at + CHUNK)
        if f == 0:
            prod[f, :, lanes] = jnp.dot(wcat[:, C2:], hid[0:C2, lanes], preferred_element_type=F32)
        else:
            prod[f, :, lanes] = jnp.dot(wcat[...], hid[:, lanes], preferred_element_type=F32)

    def act(at, first):
        lanes = slice(at, at + CHUNK)
        mean = jnp.sum(first * first, axis=0, keepdims=True) * (1.0 / C2)
        live = (col_iota((1, CHUNK)) + at) % FL < LIVE
        scale = jnp.where(live, lax.rsqrt(mean + 1e-6), 0.0)
        gain = jnp.concatenate([ghalf[...]] * (CHUNK // 128), 1)
        u = first * scale * gain
        hid[f * C2:(f + 1) * C2, lanes] = (u + u * jnp.tanh(u)).astype(BF16)

    ats = list(range(0, 4 * FL, CHUNK))
    ready = first_of(ats[0])
    for n, at in enumerate(ats):
        ahead = first_of(ats[n + 1]) if n + 1 < len(ats) else None
        act(at, ready)
        if n:
            second_of(ats[n - 1])
        if between is not None and n == 1:
            between()
        ready = ahead
    second_of(ats[-1])


def gather_taps(f, me, prod, b2col, fin, rot):
    q = col_iota((1, FL)) % PW
    bias = b2col[pl.ds(pl.multiple_of(me * CO, 8), CO), :]
    bias = jnp.concatenate([bias] * (FL // 128), 1)
    outs = []
    for a in range(2):
        for b in range(2):
            sums = {}
            for dy in range(3):
                for dx in range(3):
                    sa, sr = shift_of(a, dy - 1)
                    sb, sq = shift_of(b, dx - 1)
                    tap, ph = dy * 3 + dx, sa * 2 + sb
                    term = prod[f, tap * CO:(tap + 1) * CO, ph * FL:(ph + 1) * FL]
                    sums[sr, sq] = sums[sr, sq] + term if (sr, sq) in sums else term
            sr, sq = (-1, 1)[a], (-1, 1)[b]
            side = sums[0, sq] + pltpu.roll(sums[sr, sq], (-PW * sr) % FL, 1)
            side = pltpu.roll(side, (-sq) % FL, 1)
            side = jnp.where(q == (0 if sq < 0 else PW - 1), 0.0, side)
            outs.append(sums[0, 0] + pltpu.roll(sums[sr, 0], (-PW * sr) % FL, 1) + side + bias)
    block = col_iota((1, 128)) // 32
    for t in range(FL // 128):
        for j in range(4):
            tile = None
            for ph in range(4):
                piece = outs[ph][:, 128 * t:128 * t + 128]
                if ph != j:
                    piece = pltpu.roll(piece, (32 * (ph - j)) % 128, 1)
                tile = piece if tile is None else jnp.where(block == ph, piece, tile)
            fin[f, 4 * t + j] = tile
            parts = [tile[8 * m:8 * m + 8] for m in range(3)]
            parts = [pltpu.roll(v, 8 * m + 64 * f, 1) if m or f else v for m, v in enumerate(parts)]
            rot[f, 4 * t + j] = jnp.concatenate(parts, 0)
    fin[f, TILES - 1] = jnp.zeros((CO, 128), F32)
    rot[f, TILES - 1] = jnp.zeros((CO, 128), F32)


def mask_strips(rows, starts, tiles, keep, slots):
    lane = col_iota((8, 128))
    row = ((lane & 31) >> 3) * 2 + (lane >> 6)

    def step(to, start):
        off = start & 7
        starts[to] = start
        tiles[to] = start >> 3
        keep[to] = (row >= off).astype(jnp.int32)
        slot = ((lane >> 3) + 16 - ((off & 1) * 8 + (off >> 1))) & 15
        slots[to] = (slot >> 3) * 3 + (slot & 3)
        return start + rows[to]

    lax.fori_loop(0, N, step, 0)


def cut_strip(f, to, tiles, keep, slots, fin, rot):
    tile = tiles[to]
    first = keep[to] > 0
    one, two = fin[f, tile], fin[f, tile + 1]
    parts = [jnp.where(first, one[8 * m:8 * m + 8], two[8 * m:8 * m + 8]) for m in range(3)]
    if f == 1:
        slot = slots[to]
        tail = rot[0, tile + 1][:8]
        for n in range(1, 6):
            m = n % 3
            tail = jnp.where(slot == n, rot[n // 3, tile + 1][8 * m:8 * m + 8], tail)
        parts.append(tail)
    return jnp.concatenate(parts, 0).astype(BF16)


def strip_pick(start, count):
    shape = (9 * 16, 256)
    p, lane = row_iota(shape), col_iota(shape)
    k, col = p // 16, p % 16
    row = (start + k) % 8
    at = row % 2 * 64 + col % 2 * 32 + row // 2 * PW + col // 2 + jnp.where(k == 8, 128, 0)
    return jnp.where((lane == at) & (k < count), 1.0, 0.0).astype(BF16)


def main_kernel(
    rows_ref, tok_ref, f_ref, b1_ref, gain_ref, w_ref, b2_ref, recv0, recv1, pick,
    rows, tokv, fv, b1v, gainv, b2v, pack, tok_all, now, back, ghalf, b2col, place, wcat, xp, own, hid, prod, fin, rot, send0, send1,
    starts, tiles, keep, slots, local_sem, ok, hub_send, tok_send, tok_recv, out_sent, out_recv,
):
    me = lax.axis_index("sp")
    early = me < NF
    barrier = pltpu.get_barrier_semaphore()

    def greet(i):
        pl.semaphore_signal(barrier, inc=1, device_id=peer(i), device_id_type=MESH)

    def tok_copy(to):
        return pltpu.make_async_remote_copy(
            src_ref=pack, dst_ref=tok_all.at[me], send_sem=tok_send, recv_sem=tok_recv.at[jnp.minimum(me // 2, 4)],
            device_id=peer(to), device_id_type=MESH,
        )

    first_core = me % 2 == 0
    tok_fetch = pltpu.make_async_copy(tok_ref, tokv, local_sem.at[0])
    tok_fetch.start()

    @pl.when(early)
    def _():
        for chip in range(NF // 2):
            @pl.when(me != 2 * chip)
            def _():
                greet(2 * chip)

        for_others(me, NF, N, greet)

    @pl.when(jnp.logical_not(early))
    def _():
        greet(jnp.where(me < 10, 5, jnp.where(me < 12, 7, 1)))
        for_others(me, NF, N, greet)

    copies = [
        (f_ref.at[1], fv.at[0]), (f_ref.at[2], fv.at[1]), (b1_ref, b1v.at[0]), (gain_ref, gainv.at[0]), (b2_ref, b2v.at[0]),
        (w_ref.at[1], wcat.at[:, 0:C2]), (w_ref.at[2], wcat.at[:, C2:2 * C2]), (rows_ref, rows),
    ]
    copies = [pltpu.make_async_copy(s, d, local_sem.at[i + 1]) for i, (s, d) in enumerate(copies)]
    for copy in copies:
        copy.start()

    tok_fetch.wait()
    tokens = tokv[...].astype(F32)
    right = jnp.concatenate([tokens[HALF:], jnp.zeros((2 * HALF - TOK, 64), F32)], 0)
    block = jnp.concatenate([tokens[:HALF], right], 1).astype(BF16)
    pack[...] = block
    tok_all[me] = block

    @pl.when(early & first_core)
    def _():
        pl.semaphore_wait(barrier, NF - 1)
        pl.semaphore_signal(ok, inc=1, device_id=peer(me + 1), device_id_type=MESH)

    @pl.when(early & jnp.logical_not(first_core))
    def _():
        pl.semaphore_wait(ok, 1)

    @pl.when(me < 4)
    def _():
        for_others(NF - 1 - me, 0, NF, lambda i: tok_copy(NF - 1 - i).start())

    @pl.when((me >= 4) & early)
    def _():
        for_others(me, 0, NF, lambda i: tok_copy(i).start())

    @pl.when(jnp.logical_not(early))
    def _():
        pl.semaphore_wait(barrier, N - 1)
        for_others(me, NF, N, lambda i: tok_copy(i).start())
        for_others(me, 0, NF, lambda i: tok_copy(i).start())

    for copy in copies:
        copy.wait()

    mask_strips(rows, starts, tiles, keep, slots)
    prepare(fv, b1v, gainv, b2v, me, now, back, ghalf, b2col, place, xp)
    pick[...] = strip_pick(starts[me], rows[me])

    after = lax.rem(me + 1, N)

    def tok_wait(f, count):
        slabs = tok_all.at[pl.ds(0, count)]
        pltpu.make_async_remote_copy(
            src_ref=slabs, dst_ref=slabs, send_sem=tok_send, recv_sem=tok_recv.at[f], device_id=peer(after), device_id_type=MESH
        ).wait_recv()

    def out_copy(f, source, target, to):
        return pltpu.make_async_remote_copy(
            src_ref=source, dst_ref=target, send_sem=out_sent.at[f], recv_sem=out_recv.at[f],
            device_id=peer(to), device_id_type=MESH,
        )

    def other(i):
        twin = me + 1 - 2 * (me % 2)
        at = i + (i >= twin).astype(jnp.int32)
        return at + 1 - 2 * (at % 2)

    def out_start(f, i):
        send, recv = ((send0, recv0), (send1, recv1))[f]
        to = other(i)
        out_copy(f, send.at[to], recv.at[me], to).start()

    def finish(f):
        send, recv = ((send0, recv0), (send1, recv1))[f]
        gather_taps(f, me, prod, b2col, fin, rot)
        for i in range(N - 1):
            to = other(i)
            send[to] = cut_strip(f, to, tiles, keep, slots, fin, rot)
            if f == 1 and i >= FIRST:
                out_start(0, i)
            if f == 1 or i < FIRST:
                out_start(f, i)
        recv[me] = cut_strip(f, me, tiles, keep, slots, fin, rot)

    def hub_pass(clients, low, which):
        slabs = tok_all.at[pl.ds(low, 4 - 2 * which)]
        for to in clients:
            pltpu.make_async_remote_copy(
                src_ref=slabs, dst_ref=slabs, send_sem=hub_send, recv_sem=tok_recv.at[1 - which],
                device_id=peer(to), device_id_type=MESH,
            ).start()

    @pl.when(me == 1)
    def _():
        tok_wait(0, 1)
        tok_wait(1, 2)
        pl.semaphore_wait(barrier, 4)
        hub_pass((12, 14), 0, 0)
        tok_wait(2, 2)
        hub_pass(range(12, 16), 4, 1)
        tok_wait(3, 2)
        hub_pass(range(12, 16), 6, 1)

    @pl.when(me == 5)
    def _():
        tok_wait(2, 1)
        tok_wait(1, 2)
        pl.semaphore_wait(barrier, 2)
        hub_pass((8,), 2, 0)
        tok_wait(3, 2)
        hub_pass((8, 9), 6, 1)
        tok_wait(0, 2)
        hub_pass((8, 9), 0, 1)

    @pl.when(me == 7)
    def _():
        tok_wait(3, 1)
        tok_wait(2, 2)
        pl.semaphore_wait(barrier, 2)
        hub_pass((10,), 4, 0)
        tok_wait(1, 2)
        hub_pass((10, 11), 2, 1)
        tok_wait(0, 2)
        hub_pass((10, 11), 0, 1)

    @pl.when(early & (first_core | (me == 3)))
    def _():
        for chip in range(4):
            @pl.when(me // 2 == chip)
            def _():
                tok_wait(chip, 1)

            @pl.when(me // 2 != chip)
            def _():
                tok_wait(chip, 2)

    @pl.when(jnp.logical_not(early) & first_core)
    def _():
        tok_wait(1, 4)
        slabs = tok_all.at[pl.ds(jnp.where(me < 10, 2, jnp.where(me < 12, 4, 0)), 4)]
        pltpu.make_async_remote_copy(
            src_ref=slabs, dst_ref=slabs, send_sem=hub_send, recv_sem=tok_recv.at[0], device_id=peer(me + 1), device_id_type=MESH
        ).start()

    @pl.when(jnp.logical_not(early))
    def _():
        tok_wait(4, NF - 1)
        patches(1, tok_all, place, xp)
        convolve_own(xp, now, own)

    @pl.when(jnp.logical_not(early) & first_core)
    def _():
        tok_wait(0, 4)

    @pl.when(jnp.logical_not(early | first_core))
    def _():
        tok_wait(0, NF)

    patches(0, tok_all, place, xp)
    convolve(0, xp, now, back, own, ghalf, wcat, hid, prod)

    @pl.when(early)
    def _():
        tok_wait(4, NF)
        patches(1, tok_all, place, xp)
        convolve_own(xp, now, own)

    convolve(1, xp, now, back, own, ghalf, wcat, hid, prod, lambda: finish(0))
    finish(1)

    def tok_sent(count, sem):
        slabs = tok_all.at[pl.ds(0, count)]
        pltpu.make_async_remote_copy(
            src_ref=slabs, dst_ref=slabs, send_sem=sem, recv_sem=tok_recv.at[0], device_id=peer(after), device_id_type=MESH
        ).wait_send()

    @pl.when(early)
    def _():
        tok_sent(NF - 1, tok_send)

    @pl.when(jnp.logical_not(early))
    def _():
        tok_sent(N - 1, tok_send)

    @pl.when(me == 1)
    def _():
        tok_sent(12, hub_send)
        tok_sent(12, hub_send)

    @pl.when((me == 5) | (me == 7))
    def _():
        tok_sent(12, hub_send)

    @pl.when(jnp.logical_not(early) & first_core)
    def _():
        tok_sent(4, hub_send)

    for f, (send, recv) in enumerate(((send0, recv0), (send1, recv1))):
        out_copy(f, send.at[pl.ds(0, N - 1)], recv.at[pl.ds(0, N - 1)], after).wait()


def exchange(strip_rows, tokens, f, b1, gain, w, b2):
    hbm = pl.BlockSpec(memory_space=pltpu.HBM)
    return pl.pallas_call(
        main_kernel,
        out_shape=(pltpu.VMEM((N, CO, 128), BF16), pltpu.VMEM((N, CO + 8, 128), BF16), pltpu.VMEM((9 * 16, 256), BF16)),
        in_specs=[hbm] * 7,
        out_specs=(pl.BlockSpec(memory_space=pltpu.VMEM),) * 3,
        scratch_shapes=[
            pltpu.SMEM((N,), jnp.int32),
            pltpu.VMEM((TOK, 64), BF16),
            pltpu.VMEM((2, 144, C2), BF16),
            pltpu.VMEM((1, C2), F32),
            pltpu.VMEM((1, C2), F32),
            pltpu.VMEM((1, C2), F32),
            pltpu.VMEM((HALF, 128), BF16),
            pltpu.VMEM((N, HALF, 128), BF16),
            pltpu.VMEM((C2, 160), BF16),
            pltpu.VMEM((C2, 144), BF16),
            pltpu.VMEM((C2, 128), F32),
            pltpu.VMEM((C2, 128), F32),
            pltpu.VMEM((2, 8 * HALF, FL), BF16),
            pltpu.VMEM((9 * CO, 2 * C2), BF16),
            pltpu.VMEM((320, 4 * FL), BF16),
            pltpu.VMEM((C2, 4 * FL), F32),
            pltpu.VMEM((2 * C2, 4 * FL), BF16),
            pltpu.VMEM((FR, 9 * CO, 4 * FL), F32),
            pltpu.VMEM((FR, TILES, CO, 128), F32),
            pltpu.VMEM((FR, TILES, CO, 128), F32),
            pltpu.VMEM((N, CO, 128), BF16),
            pltpu.VMEM((N, CO + 8, 128), BF16),
            pltpu.SMEM((N,), jnp.int32),
            pltpu.SMEM((N,), jnp.int32),
            pltpu.VMEM((N, 8, 128), jnp.int32),
            pltpu.VMEM((N, 8, 128), jnp.int32),
            pltpu.SemaphoreType.DMA((9,)),
            pltpu.SemaphoreType.REGULAR,
            pltpu.SemaphoreType.DMA,
            pltpu.SemaphoreType.DMA,
            pltpu.SemaphoreType.DMA((5,)),
            pltpu.SemaphoreType.DMA((FR,)),
            pltpu.SemaphoreType.DMA((FR,)),
        ],
        compiler_params=pltpu.CompilerParams(collective_id=0, has_side_effects=True, vmem_limit_bytes=40 << 20),
    )(*(pltpu.with_memory_space_constraint(v, pltpu.HBM) for v in (strip_rows, tokens, f, b1, gain, w, b2)))


def assemble_kernel(pick, recv0, recv1, out, strips, sent):
    tail = recv1[...].astype(F32)[:, CO:]
    copies = []
    for f, recv in enumerate((recv0, recv1)):
        main = recv[...].astype(F32)[:, :CO].reshape(C2, 128)
        turns = [8 * m + 64 * f for m in range(3)]
        ninth = jnp.concatenate([pltpu.roll(tail, 128 - n, 2) if n else tail for n in turns], 1).reshape(C2, 128)
        both = jnp.concatenate([main, ninth], 1).astype(BF16)
        strip = lax.dot_general(pick[...], both, (((1,), (1,)), ((), ())), preferred_element_type=F32)
        strips[f] = strip.astype(BF16).reshape(9, 16, C2)
        copies.append(pltpu.make_async_copy(strips.at[f], out.at[0, f], sent.at[f]))
        copies[f].start()
    for copy in copies:
        copy.wait()


def assemble(pick, recv0, recv1):
    vmem = pl.BlockSpec(memory_space=pltpu.VMEM)
    return pl.pallas_call(
        assemble_kernel,
        out_shape=jax.ShapeDtypeStruct((1, FR, 9, 16, C2), BF16),
        in_specs=[vmem] * 3,
        out_specs=pl.BlockSpec(memory_space=pl.ANY),
        scratch_shapes=[pltpu.VMEM((FR, 9, 16, C2), BF16), pltpu.SemaphoreType.DMA((FR,))],
        compiler_params=pltpu.CompilerParams(vmem_limit_bytes=20 << 20),
    )(pick, recv0, recv1)


def per_device(tokens, strip_rows, first_filter, first_bias, norm_gain, second_filter, second_bias):
    f = first_filter.reshape(3, 9 * C, C2)
    w = jnp.transpose(second_filter, (0, 1, 2, 4, 3)).reshape(3, 9 * CO, C2)
    recv0, recv1, pick = exchange(strip_rows, tokens, f, first_bias, norm_gain, w, second_bias)
    return assemble(pick, recv0, recv1)


def solution(mesh):
    in_specs = (P(("req", "sp"), None), P(), P(), P(), P(), P(None, None, None, None, "sp"), P())
    out_specs = P(("req", "sp"), None, None, None, None)
    return jax.shard_map(
        per_device, mesh=mesh, in_specs=in_specs, out_specs=out_specs, check_vma=False
    )
```

```python
import jax
import jax.numpy as jnp
from jax import lax
from jax.experimental import pallas as pl
from jax.experimental.pallas import tpu as pltpu
from jax.sharding import PartitionSpec as P

C = 16
FR = 2
PH = 45
PW = 8
N = 16
NF = N // FR
FIRST = 4
TOK = FR * PH * PW // N
HALF = 24
FL = 384
LIVE = PH * PW
C2 = 384
CO = 24
TILES = 13
CHUNK = 256
MESH = pl.DeviceIdType.MESH
F32, BF16 = jnp.float32, jnp.bfloat16


def peer(i):
    return {"sp": i}


def for_others(me, low, high, act):
    def step(i, carry):
        @pl.when(i != me)
        def _():
            act(i)

        return carry

    lax.fori_loop(low, high, step, 0)


def col_iota(shape):
    return lax.broadcasted_iota(jnp.int32, shape, len(shape) - 1)


def row_iota(shape):
    return lax.broadcasted_iota(jnp.int32, shape, len(shape) - 2)


def shift_of(phase, d):
    moved = phase + d
    return moved % 2, moved // 2


def prepare(f_ref, b1_ref, gain_ref, b2_ref, me, now, back, ghalf, b2col, place, xp):
    tap1, tap2 = f_ref[0].astype(F32), f_ref[1].astype(F32)
    bias = b1_ref[...]
    hi = bias.astype(BF16).astype(F32)
    mid = (bias - hi).astype(BF16).astype(F32)
    low = bias - hi - mid
    rows = row_iota((16, C2))
    bias_rows = jnp.where(rows == 0, hi, jnp.where(rows == 1, mid, jnp.where(rows == 2, low, 0.0)))
    now[...] = jnp.concatenate([tap2, bias_rows, jnp.zeros((96, C2), F32)], 0).T[:, :160].astype(BF16)
    back[...] = jnp.concatenate([tap1, jnp.zeros((112, C2), F32)], 0).T[:, :144].astype(BF16)
    ghalf[...] = jnp.broadcast_to(gain_ref[...] * 0.5, (128, C2)).T
    b2col[...] = jnp.broadcast_to(b2_ref[...], (128, C2)).T
    shape = (8 * HALF, FL)
    token = row_iota(shape)
    src, i = token // HALF, token % HALF
    lane = col_iota(shape)
    one, zero = jnp.ones(shape, F32), jnp.zeros(shape, F32)
    place[0] = jnp.where(lane == src * TOK + i, one, zero).astype(BF16)
    place[1] = jnp.where((lane == src * TOK + HALF + i) & (i < TOK - HALF), one, zero).astype(BF16)
    xp[144:160, :] = jnp.ones((16, 4 * FL), BF16)
    xp[304:320, :] = jnp.ones((16, 4 * FL), BF16)


def patches(f, tok_all, place, xp):
    blocks = tok_all[8 * f:8 * f + 8].astype(F32).reshape(8 * HALF, 128).T.astype(BF16)
    grid = jnp.dot(blocks[:64], place[0], preferred_element_type=F32) + jnp.dot(blocks[64:], place[1], preferred_element_type=F32)
    q = col_iota((1, FL)) % PW
    for a2 in range(2):
        for b2 in range(2):
            at = (a2 * 2 + b2) * C
            field = grid[at:at + C]
            moved = {}
            for sr in ((0, -1) if a2 == 1 else (0, 1)):
                for sq in ((0, -1) if b2 == 1 else (0, 1)):
                    piece = field
                    if sr or sq:
                        piece = pltpu.roll(piece, (-(PW * sr + sq)) % FL, 1)
                    if sq:
                        piece = jnp.where(q == (0 if sq < 0 else PW - 1), 0.0, piece)
                    moved[sr, sq] = piece.astype(BF16)
            for a in range(2):
                for b in range(2):
                    for dy in range(3):
                        for dx in range(3):
                            sa, sr = shift_of(a, dy - 1)
                            sb, sq = shift_of(b, dx - 1)
                            if (sa, sb) == (a2, b2):
                                row = (160 if f == 0 else 0) + (dy * 3 + dx) * C
                                ph = a * 2 + b
                                xp[row:row + C, ph * FL:(ph + 1) * FL] = moved[sr, sq]


def convolve_own(xp, now, own):
    for at in range(0, 4 * FL, CHUNK):
        own[:, at:at + CHUNK] = jnp.dot(now[...], xp[0:160, at:at + CHUNK], preferred_element_type=F32)


def convolve(f, xp, now, back, own, ghalf, wcat, hid, prod, between=None):
    def first_of(at):
        lanes = slice(at, at + CHUNK)
        if f == 0:
            return jnp.dot(now[...], xp[160:320, lanes], preferred_element_type=F32)
        return jnp.dot(back[...], xp[160:304, lanes], preferred_element_type=F32) + own[:, lanes]

    def second_of(at):
        lanes = slice(at, at + CHUNK)
        if f == 0:
            prod[f, :, lanes] = jnp.dot(wcat[:, C2:], hid[0:C2, lanes], preferred_element_type=F32)
        else:
            prod[f, :, lanes] = jnp.dot(wcat[...], hid[:, lanes], preferred_element_type=F32)

    def act(at, first):
        lanes = slice(at, at + CHUNK)
        mean = jnp.sum(first * first, axis=0, keepdims=True) * (1.0 / C2)
        live = (col_iota((1, CHUNK)) + at) % FL < LIVE
        scale = jnp.where(live, lax.rsqrt(mean + 1e-6), 0.0)
        gain = jnp.concatenate([ghalf[...]] * (CHUNK // 128), 1)
        u = first * scale * gain
        hid[f * C2:(f + 1) * C2, lanes] = (u + u * jnp.tanh(u)).astype(BF16)

    ats = list(range(0, 4 * FL, CHUNK))
    ready = first_of(ats[0])
    for n, at in enumerate(ats):
        ahead = first_of(ats[n + 1]) if n + 1 < len(ats) else None
        if between is not None and n == 0:
            between()
        act(at, ready)
        if n:
            second_of(ats[n - 1])
        ready = ahead
    second_of(ats[-1])


def gather_taps(f, me, prod, b2col, fin, rot):
    q = col_iota((1, FL)) % PW
    bias = b2col[pl.ds(pl.multiple_of(me * CO, 8), CO), :]
    bias = jnp.concatenate([bias] * (FL // 128), 1)
    outs = []
    for a in range(2):
        for b in range(2):
            sums = {}
            for dy in range(3):
                for dx in range(3):
                    sa, sr = shift_of(a, dy - 1)
                    sb, sq = shift_of(b, dx - 1)
                    tap, ph = dy * 3 + dx, sa * 2 + sb
                    term = prod[f, tap * CO:(tap + 1) * CO, ph * FL:(ph + 1) * FL]
                    sums[sr, sq] = sums[sr, sq] + term if (sr, sq) in sums else term
            sr, sq = (-1, 1)[a], (-1, 1)[b]
            side = sums[0, sq] + pltpu.roll(sums[sr, sq], (-PW * sr) % FL, 1)
            side = pltpu.roll(side, (-sq) % FL, 1)
            side = jnp.where(q == (0 if sq < 0 else PW - 1), 0.0, side)
            outs.append(sums[0, 0] + pltpu.roll(sums[sr, 0], (-PW * sr) % FL, 1) + side + bias)
    block = col_iota((1, 128)) // 32
    for t in range(FL // 128):
        for j in range(4):
            tile = None
            for ph in range(4):
                piece = outs[ph][:, 128 * t:128 * t + 128]
                if ph != j:
                    piece = pltpu.roll(piece, (32 * (ph - j)) % 128, 1)
                tile = piece if tile is None else jnp.where(block == ph, piece, tile)
            fin[f, 4 * t + j] = tile
            parts = [tile[8 * m:8 * m + 8] for m in range(3)]
            parts = [pltpu.roll(v, 8 * m + 64 * f, 1) if m or f else v for m, v in enumerate(parts)]
            rot[f, 4 * t + j] = jnp.concatenate(parts, 0)
    fin[f, TILES - 1] = jnp.zeros((CO, 128), F32)
    rot[f, TILES - 1] = jnp.zeros((CO, 128), F32)


def mask_strips(rows, starts, tiles, keep, slots):
    lane = col_iota((8, 128))
    row = ((lane & 31) >> 3) * 2 + (lane >> 6)

    def step(to, start):
        off = start & 7
        starts[to] = start
        tiles[to] = start >> 3
        keep[to] = (row >= off).astype(jnp.int32)
        slot = ((lane >> 3) + 16 - ((off & 1) * 8 + (off >> 1))) & 15
        slots[to] = (slot >> 3) * 3 + (slot & 3)
        return start + rows[to]

    lax.fori_loop(0, N, step, 0)


def cut_strip(f, to, tiles, keep, slots, fin, rot):
    tile = tiles[to]
    first = keep[to] > 0
    one, two = fin[f, tile], fin[f, tile + 1]
    parts = [jnp.where(first, one[8 * m:8 * m + 8], two[8 * m:8 * m + 8]) for m in range(3)]
    if f == 1:
        slot = slots[to]
        tail = rot[0, tile + 1][:8]
        for n in range(1, 6):
            m = n % 3
            tail = jnp.where(slot == n, rot[n // 3, tile + 1][8 * m:8 * m + 8], tail)
        parts.append(tail)
    return jnp.concatenate(parts, 0).astype(BF16)


def strip_pick(start, count):
    shape = (9 * 16, 256)
    p, lane = row_iota(shape), col_iota(shape)
    k, col = p // 16, p % 16
    row = (start + k) % 8
    at = row % 2 * 64 + col % 2 * 32 + row // 2 * PW + col // 2 + jnp.where(k == 8, 128, 0)
    return jnp.where((lane == at) & (k < count), 1.0, 0.0).astype(BF16)


def main_kernel(
    rows_ref, tok_ref, f_ref, b1_ref, gain_ref, w_ref, b2_ref, recv0, recv1, pick,
    rows, tokv, fv, b1v, gainv, b2v, pack, tok_all, now, back, ghalf, b2col, place, wcat, xp, own, hid, prod, fin, rot, send0, send1,
    starts, tiles, keep, slots, local_sem, ok, hub_send, tok_send, tok_recv, out_sent, out_recv,
):
    me = lax.axis_index("sp")
    early = me < NF
    barrier = pltpu.get_barrier_semaphore()

    def greet(i):
        pl.semaphore_signal(barrier, inc=1, device_id=peer(i), device_id_type=MESH)

    def tok_copy(to):
        return pltpu.make_async_remote_copy(
            src_ref=pack, dst_ref=tok_all.at[me], send_sem=tok_send, recv_sem=tok_recv.at[jnp.minimum(me // 2, 4)],
            device_id=peer(to), device_id_type=MESH,
        )

    first_core = me % 2 == 0
    tok_fetch = pltpu.make_async_copy(tok_ref, tokv, local_sem.at[0])
    tok_fetch.start()

    @pl.when(early)
    def _():
        for chip in range(NF // 2):
            @pl.when(me != 2 * chip)
            def _():
                greet(2 * chip)

        for_others(me, NF, N, greet)

    @pl.when(jnp.logical_not(early))
    def _():
        greet(jnp.where(me < 10, 5, jnp.where(me < 12, 7, 1)))
        for_others(me, NF, N, greet)

    copies = [
        (f_ref.at[1], fv.at[0]), (f_ref.at[2], fv.at[1]), (b1_ref, b1v.at[0]), (gain_ref, gainv.at[0]), (b2_ref, b2v.at[0]),
        (w_ref.at[1], wcat.at[:, 0:C2]), (w_ref.at[2], wcat.at[:, C2:2 * C2]), (rows_ref, rows),
    ]
    copies = [pltpu.make_async_copy(s, d, local_sem.at[i + 1]) for i, (s, d) in enumerate(copies)]
    for copy in copies:
        copy.start()

    tok_fetch.wait()
    tokens = tokv[...].astype(F32)
    right = jnp.concatenate([tokens[HALF:], jnp.zeros((2 * HALF - TOK, 64), F32)], 0)
    block = jnp.concatenate([tokens[:HALF], right], 1).astype(BF16)
    pack[...] = block
    tok_all[me] = block

    @pl.when(early & first_core)
    def _():
        pl.semaphore_wait(barrier, NF - 1)
        pl.semaphore_signal(ok, inc=1, device_id=peer(me + 1), device_id_type=MESH)

    @pl.when(early & jnp.logical_not(first_core))
    def _():
        pl.semaphore_wait(ok, 1)

    @pl.when(me < 4)
    def _():
        for_others(NF - 1 - me, 0, NF, lambda i: tok_copy(NF - 1 - i).start())

    @pl.when((me >= 4) & early)
    def _():
        for_others(me, 0, NF, lambda i: tok_copy(i).start())

    @pl.when(jnp.logical_not(early))
    def _():
        pl.semaphore_wait(barrier, N - 1)
        for_others(me, 0, NF, lambda i: tok_copy(i).start())
        for_others(me, NF, N, lambda i: tok_copy(i).start())

    for copy in copies:
        copy.wait()

    mask_strips(rows, starts, tiles, keep, slots)
    prepare(fv, b1v, gainv, b2v, me, now, back, ghalf, b2col, place, xp)
    pick[...] = strip_pick(starts[me], rows[me])

    after = lax.rem(me + 1, N)

    def tok_wait(f, count):
        slabs = tok_all.at[pl.ds(0, count)]
        pltpu.make_async_remote_copy(
            src_ref=slabs, dst_ref=slabs, send_sem=tok_send, recv_sem=tok_recv.at[f], device_id=peer(after), device_id_type=MESH
        ).wait_recv()

    def out_copy(f, source, target, to):
        return pltpu.make_async_remote_copy(
            src_ref=source, dst_ref=target, send_sem=out_sent.at[f], recv_sem=out_recv.at[f],
            device_id=peer(to), device_id_type=MESH,
        )

    def other(i):
        twin = me + 1 - 2 * (me % 2)
        at = i + (i >= twin).astype(jnp.int32)
        return at + 1 - 2 * (at % 2)

    def out_start(f, i):
        send, recv = ((send0, recv0), (send1, recv1))[f]
        to = other(i)
        out_copy(f, send.at[to], recv.at[me], to).start()

    def finish(f):
        send, recv = ((send0, recv0), (send1, recv1))[f]
        gather_taps(f, me, prod, b2col, fin, rot)
        for i in range(N - 1):
            to = other(i)
            send[to] = cut_strip(f, to, tiles, keep, slots, fin, rot)
            if f == 1 and i >= FIRST:
                out_start(0, i)
            if f == 1 or i < FIRST:
                out_start(f, i)
        recv[me] = cut_strip(f, me, tiles, keep, slots, fin, rot)

    def hub_pass(clients, low, which):
        slabs = tok_all.at[pl.ds(low, 4 - 2 * which)]
        for to in clients:
            pltpu.make_async_remote_copy(
                src_ref=slabs, dst_ref=slabs, send_sem=hub_send, recv_sem=tok_recv.at[1 - which],
                device_id=peer(to), device_id_type=MESH,
            ).start()

    @pl.when(me == 1)
    def _():
        tok_wait(0, 1)
        tok_wait(1, 2)
        pl.semaphore_wait(barrier, 4)
        hub_pass((12, 14), 0, 0)
        tok_wait(2, 2)
        hub_pass(range(12, 16), 4, 1)
        tok_wait(3, 2)
        hub_pass(range(12, 16), 6, 1)

    @pl.when(me == 5)
    def _():
        tok_wait(2, 1)
        tok_wait(1, 2)
        pl.semaphore_wait(barrier, 2)
        hub_pass((8,), 2, 0)
        tok_wait(3, 2)
        hub_pass((8, 9), 6, 1)
        tok_wait(0, 2)
        hub_pass((8, 9), 0, 1)

    @pl.when(me == 7)
    def _():
        tok_wait(3, 1)
        tok_wait(2, 2)
        pl.semaphore_wait(barrier, 2)
        hub_pass((10,), 4, 0)
        tok_wait(1, 2)
        hub_pass((10, 11), 2, 1)
        tok_wait(0, 2)
        hub_pass((10, 11), 0, 1)

    @pl.when(early & (first_core | (me == 3)))
    def _():
        for chip in range(4):
            @pl.when(me // 2 == chip)
            def _():
                tok_wait(chip, 1)

            @pl.when(me // 2 != chip)
            def _():
                tok_wait(chip, 2)

    @pl.when(jnp.logical_not(early) & first_core)
    def _():
        tok_wait(1, 4)
        slabs = tok_all.at[pl.ds(jnp.where(me < 10, 2, jnp.where(me < 12, 4, 0)), 4)]
        pltpu.make_async_remote_copy(
            src_ref=slabs, dst_ref=slabs, send_sem=hub_send, recv_sem=tok_recv.at[0], device_id=peer(me + 1), device_id_type=MESH
        ).start()

    @pl.when(jnp.logical_not(early))
    def _():
        tok_wait(4, NF - 1)
        patches(1, tok_all, place, xp)
        convolve_own(xp, now, own)

    @pl.when(jnp.logical_not(early) & first_core)
    def _():
        tok_wait(0, 4)

    @pl.when(jnp.logical_not(early | first_core))
    def _():
        tok_wait(0, NF)

    patches(0, tok_all, place, xp)
    convolve(0, xp, now, back, own, ghalf, wcat, hid, prod)

    @pl.when(early)
    def _():
        tok_wait(4, NF)
        patches(1, tok_all, place, xp)
        convolve_own(xp, now, own)

    convolve(1, xp, now, back, own, ghalf, wcat, hid, prod, lambda: finish(0))
    finish(1)

    def tok_sent(count, sem):
        slabs = tok_all.at[pl.ds(0, count)]
        pltpu.make_async_remote_copy(
            src_ref=slabs, dst_ref=slabs, send_sem=sem, recv_sem=tok_recv.at[0], device_id=peer(after), device_id_type=MESH
        ).wait_send()

    @pl.when(early)
    def _():
        tok_sent(NF - 1, tok_send)

    @pl.when(jnp.logical_not(early))
    def _():
        tok_sent(N - 1, tok_send)

    @pl.when(me == 1)
    def _():
        tok_sent(12, hub_send)
        tok_sent(12, hub_send)

    @pl.when((me == 5) | (me == 7))
    def _():
        tok_sent(12, hub_send)

    @pl.when(jnp.logical_not(early) & first_core)
    def _():
        tok_sent(4, hub_send)

    for f, (send, recv) in enumerate(((send0, recv0), (send1, recv1))):
        out_copy(f, send.at[pl.ds(0, N - 1)], recv.at[pl.ds(0, N - 1)], after).wait()


def exchange(strip_rows, tokens, f, b1, gain, w, b2):
    hbm = pl.BlockSpec(memory_space=pltpu.HBM)
    return pl.pallas_call(
        main_kernel,
        out_shape=(pltpu.VMEM((N, CO, 128), BF16), pltpu.VMEM((N, CO + 8, 128), BF16), pltpu.VMEM((9 * 16, 256), BF16)),
        in_specs=[hbm] * 7,
        out_specs=(pl.BlockSpec(memory_space=pltpu.VMEM),) * 3,
        scratch_shapes=[
            pltpu.SMEM((N,), jnp.int32),
            pltpu.VMEM((TOK, 64), BF16),
            pltpu.VMEM((2, 144, C2), BF16),
            pltpu.VMEM((1, C2), F32),
            pltpu.VMEM((1, C2), F32),
            pltpu.VMEM((1, C2), F32),
            pltpu.VMEM((HALF, 128), BF16),
            pltpu.VMEM((N, HALF, 128), BF16),
            pltpu.VMEM((C2, 160), BF16),
            pltpu.VMEM((C2, 144), BF16),
            pltpu.VMEM((C2, 128), F32),
            pltpu.VMEM((C2, 128), F32),
            pltpu.VMEM((2, 8 * HALF, FL), BF16),
            pltpu.VMEM((9 * CO, 2 * C2), BF16),
            pltpu.VMEM((320, 4 * FL), BF16),
            pltpu.VMEM((C2, 4 * FL), F32),
            pltpu.VMEM((2 * C2, 4 * FL), BF16),
            pltpu.VMEM((FR, 9 * CO, 4 * FL), F32),
            pltpu.VMEM((FR, TILES, CO, 128), F32),
            pltpu.VMEM((FR, TILES, CO, 128), F32),
            pltpu.VMEM((N, CO, 128), BF16),
            pltpu.VMEM((N, CO + 8, 128), BF16),
            pltpu.SMEM((N,), jnp.int32),
            pltpu.SMEM((N,), jnp.int32),
            pltpu.VMEM((N, 8, 128), jnp.int32),
            pltpu.VMEM((N, 8, 128), jnp.int32),
            pltpu.SemaphoreType.DMA((9,)),
            pltpu.SemaphoreType.REGULAR,
            pltpu.SemaphoreType.DMA,
            pltpu.SemaphoreType.DMA,
            pltpu.SemaphoreType.DMA((5,)),
            pltpu.SemaphoreType.DMA((FR,)),
            pltpu.SemaphoreType.DMA((FR,)),
        ],
        compiler_params=pltpu.CompilerParams(collective_id=0, has_side_effects=True, vmem_limit_bytes=40 << 20),
    )(*(pltpu.with_memory_space_constraint(v, pltpu.HBM) for v in (strip_rows, tokens, f, b1, gain, w, b2)))


def assemble_kernel(pick, recv0, recv1, out, strips, sent):
    tail = recv1[...].astype(F32)[:, CO:]
    copies = []
    for f, recv in enumerate((recv0, recv1)):
        main = recv[...].astype(F32)[:, :CO].reshape(C2, 128)
        turns = [8 * m + 64 * f for m in range(3)]
        ninth = jnp.concatenate([pltpu.roll(tail, 128 - n, 2) if n else tail for n in turns], 1).reshape(C2, 128)
        both = jnp.concatenate([main, ninth], 1).astype(BF16)
        strip = lax.dot_general(pick[...], both, (((1,), (1,)), ((), ())), preferred_element_type=F32)
        strips[f] = strip.astype(BF16).reshape(9, 16, C2)
        copies.append(pltpu.make_async_copy(strips.at[f], out.at[0, f], sent.at[f]))
        copies[f].start()
    for copy in copies:
        copy.wait()


def assemble(pick, recv0, recv1):
    vmem = pl.BlockSpec(memory_space=pltpu.VMEM)
    return pl.pallas_call(
        assemble_kernel,
        out_shape=jax.ShapeDtypeStruct((1, FR, 9, 16, C2), BF16),
        in_specs=[vmem] * 3,
        out_specs=pl.BlockSpec(memory_space=pl.ANY),
        scratch_shapes=[pltpu.VMEM((FR, 9, 16, C2), BF16), pltpu.SemaphoreType.DMA((FR,))],
        compiler_params=pltpu.CompilerParams(vmem_limit_bytes=20 << 20),
    )(pick, recv0, recv1)


def per_device(tokens, strip_rows, first_filter, first_bias, norm_gain, second_filter, second_bias):
    f = first_filter.reshape(3, 9 * C, C2)
    w = jnp.transpose(second_filter, (0, 1, 2, 4, 3)).reshape(3, 9 * CO, C2)
    recv0, recv1, pick = exchange(strip_rows, tokens, f, first_bias, norm_gain, w, second_bias)
    return assemble(pick, recv0, recv1)


def solution(mesh):
    in_specs = (P(("req", "sp"), None), P(), P(), P(), P(), P(None, None, None, None, "sp"), P())
    out_specs = P(("req", "sp"), None, None, None, None)
    return jax.shard_map(
        per_device, mesh=mesh, in_specs=in_specs, out_specs=out_specs, check_vma=False
    )
```

```python
import jax
import jax.numpy as jnp
from jax import lax
from jax.experimental import pallas as pl
from jax.experimental.pallas import tpu as pltpu
from jax.sharding import PartitionSpec as P

C = 16
FR = 2
PH = 45
PW = 8
N = 16
NF = N // FR
FIRST = 4
TOK = FR * PH * PW // N
HALF = 24
FL = 384
LIVE = PH * PW
C2 = 384
CO = 24
TILES = 13
CHUNK = 256
MESH = pl.DeviceIdType.MESH
F32, BF16 = jnp.float32, jnp.bfloat16


def peer(i):
    return {"sp": i}


def for_others(me, low, high, act):
    def step(i, carry):
        @pl.when(i != me)
        def _():
            act(i)

        return carry

    lax.fori_loop(low, high, step, 0)


def col_iota(shape):
    return lax.broadcasted_iota(jnp.int32, shape, len(shape) - 1)


def row_iota(shape):
    return lax.broadcasted_iota(jnp.int32, shape, len(shape) - 2)


def shift_of(phase, d):
    moved = phase + d
    return moved % 2, moved // 2


def prepare(f_ref, b1_ref, gain_ref, b2_ref, me, now, back, ghalf, b2col, place, xp):
    tap1, tap2 = f_ref[0].astype(F32), f_ref[1].astype(F32)
    bias = b1_ref[...]
    hi = bias.astype(BF16).astype(F32)
    mid = (bias - hi).astype(BF16).astype(F32)
    low = bias - hi - mid
    rows = row_iota((16, C2))
    bias_rows = jnp.where(rows == 0, hi, jnp.where(rows == 1, mid, jnp.where(rows == 2, low, 0.0)))
    now[...] = jnp.concatenate([tap2, bias_rows, jnp.zeros((96, C2), F32)], 0).T[:, :160].astype(BF16)
    back[...] = jnp.concatenate([tap1, jnp.zeros((112, C2), F32)], 0).T[:, :144].astype(BF16)
    ghalf[...] = jnp.broadcast_to(gain_ref[...] * 0.5, (128, C2)).T
    b2col[...] = jnp.broadcast_to(b2_ref[...], (128, C2)).T
    shape = (8 * HALF, FL)
    token = row_iota(shape)
    src, i = token // HALF, token % HALF
    lane = col_iota(shape)
    one, zero = jnp.ones(shape, F32), jnp.zeros(shape, F32)
    place[0] = jnp.where(lane == src * TOK + i, one, zero).astype(BF16)
    place[1] = jnp.where((lane == src * TOK + HALF + i) & (i < TOK - HALF), one, zero).astype(BF16)
    xp[144:160, :] = jnp.ones((16, 4 * FL), BF16)
    xp[304:320, :] = jnp.ones((16, 4 * FL), BF16)


def patches(f, tok_all, place, xp):
    blocks = tok_all[8 * f:8 * f + 8].astype(F32).reshape(8 * HALF, 128).T.astype(BF16)
    grid = jnp.dot(blocks[:64], place[0], preferred_element_type=F32) + jnp.dot(blocks[64:], place[1], preferred_element_type=F32)
    q = col_iota((1, FL)) % PW
    for a2 in range(2):
        for b2 in range(2):
            at = (a2 * 2 + b2) * C
            field = grid[at:at + C]
            moved = {}
            for sr in ((0, -1) if a2 == 1 else (0, 1)):
                for sq in ((0, -1) if b2 == 1 else (0, 1)):
                    piece = field
                    if sr or sq:
                        piece = pltpu.roll(piece, (-(PW * sr + sq)) % FL, 1)
                    if sq:
                        piece = jnp.where(q == (0 if sq < 0 else PW - 1), 0.0, piece)
                    moved[sr, sq] = piece.astype(BF16)
            for a in range(2):
                for b in range(2):
                    for dy in range(3):
                        for dx in range(3):
                            sa, sr = shift_of(a, dy - 1)
                            sb, sq = shift_of(b, dx - 1)
                            if (sa, sb) == (a2, b2):
                                row = (160 if f == 0 else 0) + (dy * 3 + dx) * C
                                ph = a * 2 + b
                                xp[row:row + C, ph * FL:(ph + 1) * FL] = moved[sr, sq]


def convolve_own(xp, now, own):
    for at in range(0, 4 * FL, CHUNK):
        own[:, at:at + CHUNK] = jnp.dot(now[...], xp[0:160, at:at + CHUNK], preferred_element_type=F32)


def convolve(f, xp, now, back, own, ghalf, wcat, hid, prod, between=None):
    def first_of(at):
        lanes = slice(at, at + CHUNK)
        if f == 0:
            return jnp.dot(now[...], xp[160:320, lanes], preferred_element_type=F32)
        return jnp.dot(back[...], xp[160:304, lanes], preferred_element_type=F32) + own[:, lanes]

    def second_of(at):
        lanes = slice(at, at + CHUNK)
        if f == 0:
            prod[f, :, lanes] = jnp.dot(wcat[:, C2:], hid[0:C2, lanes], preferred_element_type=F32)
        else:
            prod[f, :, lanes] = jnp.dot(wcat[...], hid[:, lanes], preferred_element_type=F32)

    def act(at, first):
        lanes = slice(at, at + CHUNK)
        mean = jnp.sum(first * first, axis=0, keepdims=True) * (1.0 / C2)
        live = (col_iota((1, CHUNK)) + at) % FL < LIVE
        scale = jnp.where(live, lax.rsqrt(mean + 1e-6), 0.0)
        gain = jnp.concatenate([ghalf[...]] * (CHUNK // 128), 1)
        u = first * scale * gain
        hid[f * C2:(f + 1) * C2, lanes] = (u + u * jnp.tanh(u)).astype(BF16)

    ats = list(range(0, 4 * FL, CHUNK))
    ready = first_of(ats[0])
    for n, at in enumerate(ats):
        ahead = first_of(ats[n + 1]) if n + 1 < len(ats) else None
        if between is not None and n == 0:
            between()
        act(at, ready)
        if n:
            second_of(ats[n - 1])
        ready = ahead
    second_of(ats[-1])


def gather_taps(f, me, prod, b2col, fin, rot):
    q = col_iota((1, FL)) % PW
    bias = b2col[pl.ds(pl.multiple_of(me * CO, 8), CO), :]
    bias = jnp.concatenate([bias] * (FL // 128), 1)
    outs = []
    for a in range(2):
        for b in range(2):
            sums = {}
            for dy in range(3):
                for dx in range(3):
                    sa, sr = shift_of(a, dy - 1)
                    sb, sq = shift_of(b, dx - 1)
                    tap, ph = dy * 3 + dx, sa * 2 + sb
                    term = prod[f, tap * CO:(tap + 1) * CO, ph * FL:(ph + 1) * FL]
                    sums[sr, sq] = sums[sr, sq] + term if (sr, sq) in sums else term
            sr, sq = (-1, 1)[a], (-1, 1)[b]
            side = sums[0, sq] + pltpu.roll(sums[sr, sq], (-PW * sr) % FL, 1)
            side = pltpu.roll(side, (-sq) % FL, 1)
            side = jnp.where(q == (0 if sq < 0 else PW - 1), 0.0, side)
            outs.append(sums[0, 0] + pltpu.roll(sums[sr, 0], (-PW * sr) % FL, 1) + side + bias)
    block = col_iota((1, 128)) // 32
    for t in range(FL // 128):
        for j in range(4):
            tile = None
            for ph in range(4):
                piece = outs[ph][:, 128 * t:128 * t + 128]
                if ph != j:
                    piece = pltpu.roll(piece, (32 * (ph - j)) % 128, 1)
                tile = piece if tile is None else jnp.where(block == ph, piece, tile)
            fin[f, 4 * t + j] = tile
            parts = [tile[8 * m:8 * m + 8] for m in range(3)]
            parts = [pltpu.roll(v, 8 * m + 64 * f, 1) if m or f else v for m, v in enumerate(parts)]
            rot[f, 4 * t + j] = jnp.concatenate(parts, 0)
    fin[f, TILES - 1] = jnp.zeros((CO, 128), F32)
    rot[f, TILES - 1] = jnp.zeros((CO, 128), F32)


def mask_strips(rows, starts, tiles, keep, slots):
    lane = col_iota((8, 128))
    row = ((lane & 31) >> 3) * 2 + (lane >> 6)

    def step(to, start):
        off = start & 7
        starts[to] = start
        tiles[to] = start >> 3
        keep[to] = (row >= off).astype(jnp.int32)
        slot = ((lane >> 3) + 16 - ((off & 1) * 8 + (off >> 1))) & 15
        slots[to] = (slot >> 3) * 3 + (slot & 3)
        return start + rows[to]

    lax.fori_loop(0, N, step, 0)


def cut_strip(f, to, tiles, keep, slots, fin, rot):
    tile = tiles[to]
    first = keep[to] > 0
    one, two = fin[f, tile], fin[f, tile + 1]
    parts = [jnp.where(first, one[8 * m:8 * m + 8], two[8 * m:8 * m + 8]) for m in range(3)]
    if f == 1:
        slot = slots[to]
        tail = rot[0, tile + 1][:8]
        for n in range(1, 6):
            m = n % 3
            tail = jnp.where(slot == n, rot[n // 3, tile + 1][8 * m:8 * m + 8], tail)
        parts.append(tail)
    return jnp.concatenate(parts, 0).astype(BF16)


def strip_pick(start, count):
    shape = (9 * 16, 256)
    p, lane = row_iota(shape), col_iota(shape)
    k, col = p // 16, p % 16
    row = (start + k) % 8
    at = row % 2 * 64 + col % 2 * 32 + row // 2 * PW + col // 2 + jnp.where(k == 8, 128, 0)
    return jnp.where((lane == at) & (k < count), 1.0, 0.0).astype(BF16)


def main_kernel(
    rows_ref, tok_ref, f_ref, b1_ref, gain_ref, w_ref, b2_ref, recv0, recv1, pick,
    rows, tokv, fv, b1v, gainv, b2v, pack, tok_all, now, back, ghalf, b2col, place, wcat, xp, own, hid, prod, fin, rot, send0, send1,
    starts, tiles, keep, slots, local_sem, ok, hub_send, tok_send, tok_recv, out_sent, out_recv,
):
    me = lax.axis_index("sp")
    early = me < NF
    barrier = pltpu.get_barrier_semaphore()

    def greet(i):
        pl.semaphore_signal(barrier, inc=1, device_id=peer(i), device_id_type=MESH)

    def tok_copy(to):
        return pltpu.make_async_remote_copy(
            src_ref=pack, dst_ref=tok_all.at[me], send_sem=tok_send, recv_sem=tok_recv.at[jnp.minimum(me // 2, 4)],
            device_id=peer(to), device_id_type=MESH,
        )

    first_core = me % 2 == 0
    tok_fetch = pltpu.make_async_copy(tok_ref, tokv, local_sem.at[0])
    tok_fetch.start()

    @pl.when(early)
    def _():
        for chip in range(NF // 2):
            @pl.when(me != 2 * chip)
            def _():
                greet(2 * chip)

        for_others(me, NF, N, greet)

    @pl.when(jnp.logical_not(early))
    def _():
        greet(jnp.where(me < 10, 5, jnp.where(me < 12, 7, 1)))
        for_others(me, NF, N, greet)

    copies = [
        (f_ref.at[1], fv.at[0]), (f_ref.at[2], fv.at[1]), (b1_ref, b1v.at[0]), (gain_ref, gainv.at[0]), (b2_ref, b2v.at[0]),
        (w_ref.at[1], wcat.at[:, 0:C2]), (w_ref.at[2], wcat.at[:, C2:2 * C2]), (rows_ref, rows),
    ]
    copies = [pltpu.make_async_copy(s, d, local_sem.at[i + 1]) for i, (s, d) in enumerate(copies)]
    for copy in copies:
        copy.start()

    tok_fetch.wait()
    tokens = tokv[...].astype(F32)
    right = jnp.concatenate([tokens[HALF:], jnp.zeros((2 * HALF - TOK, 64), F32)], 0)
    block = jnp.concatenate([tokens[:HALF], right], 1).astype(BF16)
    pack[...] = block
    tok_all[me] = block

    @pl.when(early & first_core)
    def _():
        pl.semaphore_wait(barrier, NF - 1)
        pl.semaphore_signal(ok, inc=1, device_id=peer(me + 1), device_id_type=MESH)

    @pl.when(early & jnp.logical_not(first_core))
    def _():
        pl.semaphore_wait(ok, 1)

    @pl.when(me < 4)
    def _():
        for_others(NF - 1 - me, 0, NF, lambda i: tok_copy(NF - 1 - i).start())

    @pl.when((me >= 4) & early)
    def _():
        for_others(me, 0, NF, lambda i: tok_copy(i).start())

    @pl.when(jnp.logical_not(early))
    def _():
        pl.semaphore_wait(barrier, N - 1)
        for_others(me, 0, NF, lambda i: tok_copy(i).start())
        for_others(me, NF, N, lambda i: tok_copy(i).start())

    for copy in copies:
        copy.wait()

    mask_strips(rows, starts, tiles, keep, slots)
    prepare(fv, b1v, gainv, b2v, me, now, back, ghalf, b2col, place, xp)
    pick[...] = strip_pick(starts[me], rows[me])

    after = lax.rem(me + 1, N)

    def tok_wait(f, count):
        slabs = tok_all.at[pl.ds(0, count)]
        pltpu.make_async_remote_copy(
            src_ref=slabs, dst_ref=slabs, send_sem=tok_send, recv_sem=tok_recv.at[f], device_id=peer(after), device_id_type=MESH
        ).wait_recv()

    def out_copy(f, source, target, to):
        return pltpu.make_async_remote_copy(
            src_ref=source, dst_ref=target, send_sem=out_sent.at[f], recv_sem=out_recv.at[f],
            device_id=peer(to), device_id_type=MESH,
        )

    def other(i):
        twin = me + 1 - 2 * (me % 2)
        at = i + (i >= twin).astype(jnp.int32)
        return at + 1 - 2 * (at % 2)

    def out_start(f, i):
        send, recv = ((send0, recv0), (send1, recv1))[f]
        to = other(i)
        out_copy(f, send.at[to], recv.at[me], to).start()

    def finish(f):
        send, recv = ((send0, recv0), (send1, recv1))[f]
        gather_taps(f, me, prod, b2col, fin, rot)
        for i in range(N - 1):
            to = other(i)
            send[to] = cut_strip(f, to, tiles, keep, slots, fin, rot)
            if f == 1 and i >= FIRST:
                out_start(0, i)
            if f == 1 or i < FIRST:
                out_start(f, i)
        recv[me] = cut_strip(f, me, tiles, keep, slots, fin, rot)

    def hub_pass(clients, low, which):
        slabs = tok_all.at[pl.ds(low, 4 - 2 * which)]
        for to in clients:
            pltpu.make_async_remote_copy(
                src_ref=slabs, dst_ref=slabs, send_sem=hub_send, recv_sem=tok_recv.at[1 - which],
                device_id=peer(to), device_id_type=MESH,
            ).start()

    @pl.when(me == 1)
    def _():
        tok_wait(0, 1)
        tok_wait(1, 2)
        pl.semaphore_wait(barrier, 4)
        hub_pass((14, 12), 0, 0)
        tok_wait(2, 2)
        hub_pass((14, 15, 12, 13), 4, 1)
        tok_wait(3, 2)
        hub_pass((14, 15, 12, 13), 6, 1)

    @pl.when(me == 5)
    def _():
        tok_wait(2, 1)
        tok_wait(1, 2)
        pl.semaphore_wait(barrier, 2)
        hub_pass((8,), 2, 0)
        tok_wait(3, 2)
        hub_pass((8, 9), 6, 1)
        tok_wait(0, 2)
        hub_pass((8, 9), 0, 1)

    @pl.when(me == 7)
    def _():
        tok_wait(3, 1)
        tok_wait(2, 2)
        pl.semaphore_wait(barrier, 2)
        hub_pass((10,), 4, 0)
        tok_wait(1, 2)
        hub_pass((10, 11), 2, 1)
        tok_wait(0, 2)
        hub_pass((10, 11), 0, 1)

    @pl.when(early & (first_core | (me == 3)))
    def _():
        for chip in range(4):
            @pl.when(me // 2 == chip)
            def _():
                tok_wait(chip, 1)

            @pl.when(me // 2 != chip)
            def _():
                tok_wait(chip, 2)

    @pl.when(jnp.logical_not(early) & first_core)
    def _():
        tok_wait(1, 4)
        slabs = tok_all.at[pl.ds(jnp.where(me < 10, 2, jnp.where(me < 12, 4, 0)), 4)]
        pltpu.make_async_remote_copy(
            src_ref=slabs, dst_ref=slabs, send_sem=hub_send, recv_sem=tok_recv.at[0], device_id=peer(me + 1), device_id_type=MESH
        ).start()

    @pl.when(jnp.logical_not(early))
    def _():
        tok_wait(4, NF - 1)
        patches(1, tok_all, place, xp)
        convolve_own(xp, now, own)

    @pl.when(jnp.logical_not(early) & first_core)
    def _():
        tok_wait(0, 4)

    @pl.when(jnp.logical_not(early | first_core))
    def _():
        tok_wait(0, NF)

    patches(0, tok_all, place, xp)
    convolve(0, xp, now, back, own, ghalf, wcat, hid, prod)

    @pl.when(early)
    def _():
        tok_wait(4, NF)
        patches(1, tok_all, place, xp)
        convolve_own(xp, now, own)

    convolve(1, xp, now, back, own, ghalf, wcat, hid, prod, lambda: finish(0))
    finish(1)

    def tok_sent(count, sem):
        slabs = tok_all.at[pl.ds(0, count)]
        pltpu.make_async_remote_copy(
            src_ref=slabs, dst_ref=slabs, send_sem=sem, recv_sem=tok_recv.at[0], device_id=peer(after), device_id_type=MESH
        ).wait_send()

    @pl.when(early)
    def _():
        tok_sent(NF - 1, tok_send)

    @pl.when(jnp.logical_not(early))
    def _():
        tok_sent(N - 1, tok_send)

    @pl.when(me == 1)
    def _():
        tok_sent(12, hub_send)
        tok_sent(12, hub_send)

    @pl.when((me == 5) | (me == 7))
    def _():
        tok_sent(12, hub_send)

    @pl.when(jnp.logical_not(early) & first_core)
    def _():
        tok_sent(4, hub_send)

    for f, (send, recv) in enumerate(((send0, recv0), (send1, recv1))):
        out_copy(f, send.at[pl.ds(0, N - 1)], recv.at[pl.ds(0, N - 1)], after).wait()


def exchange(strip_rows, tokens, f, b1, gain, w, b2):
    hbm = pl.BlockSpec(memory_space=pltpu.HBM)
    return pl.pallas_call(
        main_kernel,
        out_shape=(pltpu.VMEM((N, CO, 128), BF16), pltpu.VMEM((N, CO + 8, 128), BF16), pltpu.VMEM((9 * 16, 256), BF16)),
        in_specs=[hbm] * 7,
        out_specs=(pl.BlockSpec(memory_space=pltpu.VMEM),) * 3,
        scratch_shapes=[
            pltpu.SMEM((N,), jnp.int32),
            pltpu.VMEM((TOK, 64), BF16),
            pltpu.VMEM((2, 144, C2), BF16),
            pltpu.VMEM((1, C2), F32),
            pltpu.VMEM((1, C2), F32),
            pltpu.VMEM((1, C2), F32),
            pltpu.VMEM((HALF, 128), BF16),
            pltpu.VMEM((N, HALF, 128), BF16),
            pltpu.VMEM((C2, 160), BF16),
            pltpu.VMEM((C2, 144), BF16),
            pltpu.VMEM((C2, 128), F32),
            pltpu.VMEM((C2, 128), F32),
            pltpu.VMEM((2, 8 * HALF, FL), BF16),
            pltpu.VMEM((9 * CO, 2 * C2), BF16),
            pltpu.VMEM((320, 4 * FL), BF16),
            pltpu.VMEM((C2, 4 * FL), F32),
            pltpu.VMEM((2 * C2, 4 * FL), BF16),
            pltpu.VMEM((FR, 9 * CO, 4 * FL), F32),
            pltpu.VMEM((FR, TILES, CO, 128), F32),
            pltpu.VMEM((FR, TILES, CO, 128), F32),
            pltpu.VMEM((N, CO, 128), BF16),
            pltpu.VMEM((N, CO + 8, 128), BF16),
            pltpu.SMEM((N,), jnp.int32),
            pltpu.SMEM((N,), jnp.int32),
            pltpu.VMEM((N, 8, 128), jnp.int32),
            pltpu.VMEM((N, 8, 128), jnp.int32),
            pltpu.SemaphoreType.DMA((9,)),
            pltpu.SemaphoreType.REGULAR,
            pltpu.SemaphoreType.DMA,
            pltpu.SemaphoreType.DMA,
            pltpu.SemaphoreType.DMA((5,)),
            pltpu.SemaphoreType.DMA((FR,)),
            pltpu.SemaphoreType.DMA((FR,)),
        ],
        compiler_params=pltpu.CompilerParams(collective_id=0, has_side_effects=True, vmem_limit_bytes=40 << 20),
    )(*(pltpu.with_memory_space_constraint(v, pltpu.HBM) for v in (strip_rows, tokens, f, b1, gain, w, b2)))


def assemble_kernel(pick, recv0, recv1, out, strips, sent):
    tail = recv1[...].astype(F32)[:, CO:]
    copies = []
    for f, recv in enumerate((recv0, recv1)):
        main = recv[...].astype(F32)[:, :CO].reshape(C2, 128)
        turns = [8 * m + 64 * f for m in range(3)]
        ninth = jnp.concatenate([pltpu.roll(tail, 128 - n, 2) if n else tail for n in turns], 1).reshape(C2, 128)
        both = jnp.concatenate([main, ninth], 1).astype(BF16)
        strip = lax.dot_general(pick[...], both, (((1,), (1,)), ((), ())), preferred_element_type=F32)
        strips[f] = strip.astype(BF16).reshape(9, 16, C2)
        copies.append(pltpu.make_async_copy(strips.at[f], out.at[0, f], sent.at[f]))
        copies[f].start()
    for copy in copies:
        copy.wait()


def assemble(pick, recv0, recv1):
    vmem = pl.BlockSpec(memory_space=pltpu.VMEM)
    return pl.pallas_call(
        assemble_kernel,
        out_shape=jax.ShapeDtypeStruct((1, FR, 9, 16, C2), BF16),
        in_specs=[vmem] * 3,
        out_specs=pl.BlockSpec(memory_space=pl.ANY),
        scratch_shapes=[pltpu.VMEM((FR, 9, 16, C2), BF16), pltpu.SemaphoreType.DMA((FR,))],
        compiler_params=pltpu.CompilerParams(vmem_limit_bytes=20 << 20),
    )(pick, recv0, recv1)


def per_device(tokens, strip_rows, first_filter, first_bias, norm_gain, second_filter, second_bias):
    f = first_filter.reshape(3, 9 * C, C2)
    w = jnp.transpose(second_filter, (0, 1, 2, 4, 3)).reshape(3, 9 * CO, C2)
    recv0, recv1, pick = exchange(strip_rows, tokens, f, first_bias, norm_gain, w, second_bias)
    return assemble(pick, recv0, recv1)


def solution(mesh):
    in_specs = (P(("req", "sp"), None), P(), P(), P(), P(), P(None, None, None, None, "sp"), P())
    out_specs = P(("req", "sp"), None, None, None, None)
    return jax.shard_map(
        per_device, mesh=mesh, in_specs=in_specs, out_specs=out_specs, check_vma=False
    )
```
